32 devices in a mesh: section: 2 (over core), dp: 16 (over z, y, x).
Axes of the slice: x: 2, y: 2, z: 4, core: 2. Of those that a mesh axis runs over, the one named last changes fastest.
Arguments:
- inputs: bfloat16 [8, 16, 32, 64, 128], P(None, 'dp'), may hold values from -66 to 66
- channel_mean: float32 [128], replicated, may hold values from -3 to 3
- channel_std: float32 [128], replicated, may hold values from 0.5 to 2
- cotangent: bfloat16 [8, 16, 32, 64, 128], P(None, 'dp'), may hold values from -15 to 15
- conv_w1: bfloat16 [2, 3, 3, 128, 128], P('section'), may hold values from -0.1875 to 0.1875
- conv_b1: float32 [2, 128], P('section'), may hold values from -3 to 3
- bn_gain1: float32 [2, 128], P('section'), may hold values from 0.25 to 1.75
- bn_shift1: float32 [2, 128], P('section'), may hold values from -3 to 3
- conv_w2: bfloat16 [2, 3, 3, 128, 128], P('section'), may hold values from -0.1875 to 0.1875
- conv_b2: float32 [2, 128], P('section'), may hold values from -3 to 3
- bn_gain2: float32 [2, 128], P('section'), may hold values from 0.25 to 1.75
- bn_shift2: float32 [2, 128], P('section'), may hold values from -3 to 3
Outputs:
- block_outputs: bfloat16 [2, 8, 16, 32, 64, 128], P('section', None, 'dp')
- edge_grads: bfloat16 [2, 8, 16, 32, 64, 128], P('section', None, 'dp')
- grad_w1: float32 [2, 3, 3, 128, 128], P('section')
- grad_b1: float32 [2, 128], P('section')
- grad_gain1: float32 [2, 128], P('section')
- grad_shift1: float32 [2, 128], P('section')
- grad_w2: float32 [2, 3, 3, 128, 128], P('section')
- grad_b2: float32 [2, 128], P('section')
- grad_gain2: float32 [2, 128], P('section')
- grad_shift2: float32 [2, 128], P('section')
The draws below stay inside these ranges and needn't reach their ends.
All inputs are finite; a program needn't handle non-finite values.
Results may differ from the reference program's by a relative error of at most 0.011.
Values may be sent and summed in bfloat16 or wider, within the bound.
A program may use at most 128 MiB of HBM per device.

```python
import math
import jax
import jax.numpy as jnp
from jax import lax

C = 128
H = 32
W = 64
MB = 8
SAMPLES = 16


def draw_inputs(key, part):
    key = jax.random.fold_in(key, 11)
    key_chan, key_jit, key_off, key_noise = jax.random.split(key, 4)
    ramp_rows = 1.0 + 2.0 * jnp.arange(SAMPLES, dtype=jnp.float32) / max(SAMPLES - 1, 1)
    chan_scale = jnp.exp(jax.random.uniform(key_chan, (C,), jnp.float32, -0.7, 0.7))
    jitter = jnp.exp(jax.random.uniform(key_jit, (MB, SAMPLES), jnp.float32, -0.3, 0.3))
    offsets = jnp.clip(jax.random.normal(key_off, (MB, SAMPLES, 1, 1, C), jnp.float32), -3.0, 3.0)
    noise_part = jnp.clip(jax.random.normal(key_noise, (MB, SAMPLES, H, W, C), jnp.float32), -5.0, 5.0)
    row_level = (ramp_rows[None, :] * jitter)[:, :, None, None, None]
    return (row_level * chan_scale * (offsets + noise_part)).astype(jnp.bfloat16)


def draw_cotangent(key, part):
    key = jax.random.fold_in(key, 23)
    ramp_rows = 1.0 + 2.0 * jnp.arange(SAMPLES, dtype=jnp.float32) / max(SAMPLES - 1, 1)
    noise_part = jnp.clip(jax.random.normal(key, (MB, SAMPLES, H, W, C), jnp.float32), -5.0, 5.0)
    return (ramp_rows[None, :, None, None, None] * noise_part).astype(jnp.bfloat16)


def shard_levels(own_key, dims, shards, low, largest):
    level, own = 1.0, jax.random.fold_in(own_key, 6)
    for axis_at, shards_of in shards:
        heights = jnp.exp(jax.random.uniform(jax.random.fold_in(own, axis_at), (shards_of,), jnp.float32, low / len(shards), largest / len(shards)))
        level = level * jnp.repeat(heights, dims[axis_at] // shards_of).reshape([-1 if axis == axis_at else 1 for axis in range(len(dims))])
    return level


def centred(stream_key, dims, scale, bound, cuts=(), kind=jnp.bfloat16):
    level = shard_levels(stream_key, dims, cuts, -0.22, 0.18) if cuts else 1.0
    entries = jax.random.normal(stream_key, dims, jnp.float32) * scale * level
    return jnp.minimum(jnp.maximum(entries, -bound), bound).astype(kind)


def setup_inputs(seed: int = 0) -> dict:
    arg_keys = jax.random.split(jax.random.key(seed), 13)
    return {
        "inputs": draw_inputs(jax.random.fold_in(arg_keys[12], 71), 0),
        "channel_mean": centred(arg_keys[1], (C,), 1.0, 3.0, (), jnp.float32),
        "channel_std": jnp.clip(jnp.exp(jax.random.uniform(arg_keys[2], (C,), jnp.float32, math.log(0.5), math.log(2.0))), 0.5, 2.0),
        "cotangent": draw_cotangent(jax.random.fold_in(arg_keys[12], 71), 0),
        "conv_w1": centred(arg_keys[4], (2, 3, 3, C, C), (9 * C) ** -0.5, 0.1875, ((0, 2),)),
        "conv_b1": centred(arg_keys[5], (2, C), 0.5, 3.0, ((0, 2),), jnp.float32),
        "bn_gain1": jnp.clip(1.0 + 0.15 * jax.random.normal(arg_keys[6], (2, C), jnp.float32), 0.25, 1.75),
        "bn_shift1": centred(arg_keys[7], (2, C), 0.5, 3.0, ((0, 2),), jnp.float32),
        "conv_w2": centred(arg_keys[8], (2, 3, 3, C, C), (9 * C) ** -0.5, 0.1875, ((0, 2),)),
        "conv_b2": centred(arg_keys[9], (2, C), 0.5, 3.0, ((0, 2),), jnp.float32),
        "bn_gain2": jnp.clip(1.0 + 0.15 * jax.random.normal(arg_keys[10], (2, C), jnp.float32), 0.25, 1.75),
        "bn_shift2": centred(arg_keys[11], (2, C), 0.5, 3.0, ((0, 2),), jnp.float32),
    }


norm_eps = 1e-05

@jax.custom_vjp
def low(v):
    return lax.optimization_barrier(v.astype(jnp.bfloat16)).astype(jnp.float32)

@jax.custom_vjp
def low_back(v):
    return v

def low_keep(v):
    return (low(v), None)

def low_pass(kept, grad):
    return (grad,)

def back_keep(v):
    return (v, None)

def back_low(kept, grad):
    return (low(grad),)
low.defvjp(low_keep, low_pass)
low_back.defvjp(back_keep, back_low)

def pad_grid(field_in):
    wrapped = jnp.concatenate([field_in[:, :, -1:], field_in, field_in[:, :, :1]], axis=2)
    return jnp.pad(wrapped, ((0, 0), (1, 1), (0, 0), (0, 0)))

def conv_high(field_in, kernel):
    return lax.conv_general_dilated(pad_grid(field_in), kernel, (1, 1), 'VALID', dimension_numbers=('NHWC', 'HWIO', 'NHWC'), precision=lax.Precision.HIGHEST)

def batch_norm(activ, gain, shift_vec):
    center = lax.optimization_barrier(jnp.mean(activ, axis=(0, 1, 2)))
    spread = lax.rsqrt(lax.optimization_barrier(jnp.mean(activ * activ, axis=(0, 1, 2))) - center * center + norm_eps)
    return (activ - center) * spread * gain + shift_vec

def res_block(skip_in, weights):
    w_one, b_one, g_one, s_one, w_two, b_two, g_two, s_two = weights
    pre_one = low_back(conv_high(low(skip_in), w_one)) + b_one
    normed_one = batch_norm(jax.nn.silu(pre_one), g_one, s_one)
    pre_two = low_back(conv_high(low(normed_one), w_two)) + b_two
    return skip_in + batch_norm(jax.nn.silu(pre_two), g_two, s_two)

def reference(inputs, channel_mean, channel_std, cotangent, conv_w1, conv_b1, bn_gain1, bn_shift1, conv_w2, conv_b2, bn_gain2, bn_shift2):
    weights = (conv_w1.astype(jnp.float32), conv_b1, bn_gain1, bn_shift1, conv_w2.astype(jnp.float32), conv_b2, bn_gain2, bn_shift2)
    raw_in = inputs.astype(jnp.float32)
    probe_in = jnp.zeros(raw_in.shape, jnp.float32)

    def whole_net(weight_set, raw_all, probe_all):
        first_set = tuple((w_item[0] for w_item in weight_set))
        second_set = tuple((w_item[1] for w_item in weight_set))

        def one_batch(pair_in):
            raw_mb, probe_mb = pair_in
            sent_out = low(low_back(res_block((raw_mb - channel_mean) / channel_std, first_set)))
            return (sent_out, res_block(sent_out + probe_mb, second_set))
        return lax.map(jax.checkpoint(one_batch), (raw_all, probe_all))
    (sent_out, final_out), pull_back = jax.vjp(whole_net, weights, raw_in, probe_in)
    grad_set, grad_raw, grad_probe = pull_back((jnp.zeros_like(sent_out), cotangent.astype(jnp.float32)))
    block_outputs = jnp.stack([sent_out, final_out]).astype(jnp.bfloat16)
    edge_grads = jnp.stack([grad_raw, grad_probe]).astype(jnp.bfloat16)
    return (block_outputs, edge_grads, grad_set[0], grad_set[1], grad_set[2], grad_set[3], grad_set[4], grad_set[5], grad_set[6], grad_set[7])
```

```python
import functools

import jax
import jax.numpy as jnp
from jax import lax
from jax.experimental import pallas as pl
from jax.experimental.pallas import tpu as pltpu
from jax.sharding import PartitionSpec as P

norm_eps = 1e-05
MESH = pl.DeviceIdType.MESH
bf16 = jnp.bfloat16
f32 = jnp.float32
C = 128
CHUNK = 2


def dot(a, b):
    return jnp.dot(a, b, preferred_element_type=f32)


def twice(v):
    return jnp.concatenate([v, v], axis=-1)


def fold_rows(v):
    one = jnp.sum(v, axis=0, keepdims=True)
    return one[:, :C] + one[:, C:]


def kernel(n, grp, *refs):
    (
        inp, cot, mean, std, w1, b1, g1, s1, w2, b2, g2, s2,
        bo, eg, gw1, gw2, gvec,
        XIN, COT, DY0, XC, LB, HS, DN, WF, WD, ACC, WR, PV, ST, VACC, VR,
        MSG, SLOT, GF, GS, GR0, GR1, GQ, GS2, GR2, GO,
        isem, wlsem, wssem, wrsem, msend, mrecv, olsem, ossem, orsem, gsend, grecv, vsem,
    ) = refs
    micro = inp.shape[0]
    half = micro // 2
    Q = inp.shape[1]
    W = inp.shape[3]
    rows = Q * W
    count = float(2 * rows * n)
    B = grp
    A = n // B
    PR = GF.shape[2]

    me = lax.axis_index("dp")
    sec = lax.axis_index("section")
    sib = 1 - sec
    ga = me // B
    gb = me % B

    barrier = pltpu.get_barrier_semaphore()

    def greet(i, carry):
        pl.semaphore_signal(barrier, inc=1, device_id={"dp": lax.rem(me + i, n)}, device_id_type=MESH)
        return carry

    lax.fori_loop(1, n, greet, 0)
    pl.semaphore_signal(barrier, inc=1, device_id={"section": sib}, device_id_type=MESH)

    for m in range(half):
        for e in range(2):
            lanes = pl.ds(e * C, C)
            pltpu.make_async_copy(inp.at[sec * half + m, :, e], XIN.at[m, :, :, lanes], isem.at[m]).start()
    for m in range(half):
        for e in range(2):
            lanes = pl.ds(e * C, C)
            pltpu.make_async_copy(cot.at[sec * half + m, :, e], COT.at[m, :, :, lanes], isem.at[half + m]).start()
    for v, ref in enumerate((w1, w2)):
        pltpu.make_async_copy(ref, WR.at[sec, v], wlsem.at[v]).start()

    for v, ref in enumerate((b1, g1, s1, b2, g2, s2)):
        PV[sec, v : v + 1] = ref[...]

    halo = jnp.zeros((W, C), bf16)
    for j in range(3):
        LB[j, 0, :, 0:C] = halo
        LB[j, Q, :, C : 2 * C] = halo

    def zero_halo(i, carry):
        XC[i, 0, :, 0:C] = halo
        XC[i, Q, :, C : 2 * C] = halo
        return carry

    lax.fori_loop(0, 4 * half, zero_halo, 0)
    for i in range(4):
        ACC[i] = jnp.zeros(ACC.shape[1:], f32)
    VACC[...] = jnp.zeros(VACC.shape, f32)
    GF[...] = jnp.zeros(GF.shape, f32)

    pl.semaphore_wait(barrier, n)

    for v in range(2):
        pltpu.make_async_copy(w1, WR.at[sec, v], wlsem.at[v]).wait()
    for v in range(2):
        pltpu.make_async_remote_copy(
            WR.at[sec, v], WR.at[sec, v], wssem.at[v], wrsem.at[v], device_id={"section": sib}, device_id_type=MESH
        ).start()
    pltpu.make_async_remote_copy(
        PV.at[sec], PV.at[sec], wssem.at[2], wrsem.at[2], device_id={"section": sib}, device_id_type=MESH
    ).start()

    def prep(b, v):
        for j in range(3):
            for t in range(2):
                for s in range(2):
                    for e in range(2):
                        i = 2 * t + s - e
                        r, c = slice(s * C, s * C + C), slice(e * C, e * C + C)
                        if 0 <= i <= 2:
                            WF[b * 2 + v, j, t, r, c] = (WR[b, v, i * 3 + j].astype(f32) * 0.5).astype(bf16)
                            WD[b * 2 + v, j, t, r, c] = WR[b, v, (2 - i) * 3 + 2 - j].T
                        else:
                            WF[b * 2 + v, j, t, r, c] = jnp.zeros((C, C), bf16)
                            WD[b * 2 + v, j, t, r, c] = jnp.zeros((C, C), bf16)

    def vec(b, v):
        return PV[b, v : v + 1]

    def send_sums(i, *sums):
        for r, v in enumerate(sums):
            MSG[i, r : r + 1] = v
        SLOT[i, me] = MSG[i]

        def one(d, carry):
            pltpu.make_async_remote_copy(
                MSG.at[i], SLOT.at[i, me], msend.at[i], mrecv.at[i],
                device_id={"dp": lax.rem(me + d, n)}, device_id_type=MESH,
            ).start()
            return carry

        lax.fori_loop(1, n, one, 0)

    def take_sums(i):
        if n > 1:
            many = SLOT.at[i, pl.ds(0, n - 1)]
            pltpu.make_async_copy(many, many, mrecv.at[i]).wait()
            pltpu.make_async_copy(many, many, msend.at[i]).wait()
        total = SLOT[i, 0]
        for d in range(1, n):
            total = total + SLOT[i, d]
        return total

    def norm_forward(b, v, m, total):
        mu = total[0:1] / count
        rstd = lax.rsqrt(total[1:2] / count - mu * mu + norm_eps)
        ST[b * 2 + v, m, 0:1] = mu
        ST[b * 2 + v, m, 1:2] = rstd
        sc = vec(b, 1 + 3 * v) * rstd
        return twice(sc), twice(vec(b, 2 + 3 * v) - mu * sc)

    def norm_backward(b, v, m, shift_sum, prod_sum):
        mu = ST[b * 2 + v, m, 0:1]
        rstd = ST[b * 2 + v, m, 1:2]
        gain_sum = rstd * (prod_sum - mu * shift_sum)
        VACC[b, 3 * v + 1 : 3 * v + 2] += gain_sum
        VACC[b, 3 * v + 2 : 3 * v + 3] += shift_sum
        ca = vec(b, 1 + 3 * v) * rstd
        cc = -ca * rstd * gain_sum / count
        cb = -ca * shift_sum / count - cc * mu
        return twice(ca), twice(cb), twice(cc)

    def put(center, q, v):
        k = v.shape[0]
        for j in range(3):
            u = (v if j == 1 else pltpu.roll(v, 1 if j == 0 else W - 1, 1)).astype(bf16)
            ref = center if j == 1 else LB.at[j]
            ref[q : q + k, :, C : 2 * C] = u[:, :, :C]
            ref[q + 1 : q + k + 1, :, 0:C] = u[:, :, C:]

    def get(center, q, k):
        return jnp.concatenate([center[q : q + k, :, C : 2 * C], center[q + 1 : q + k + 1, :, 0:C]], axis=-1)

    def conv(center, w):
        acc = None
        for j in range(3):
            ref = center if j == 1 else LB.at[j]
            for t in range(2):
                d = dot(ref[t : t + Q].reshape(rows, 2 * C), w[j, t])
                acc = d if acc is None else acc + d
        return acc

    def wgrad(i, center):
        left = jnp.concatenate([center[0:Q].reshape(rows, 2 * C), center[1 : Q + 1].reshape(rows, 2 * C)], axis=-1)
        right = jnp.concatenate([get(LB.at[j], 0, Q).reshape(rows, 2 * C) for j in range(3)], axis=-1)
        ACC[i] += lax.dot_general(left, right, (((0,), (0,)), ((), ())), preferred_element_type=f32)

    def chunks():
        return range(0, Q, CHUNK)

    def part(r, q):
        return r[q * W : (q + CHUNK) * W].reshape(CHUNK, W, 2 * C)

    def add8(total, v):
        return total + jnp.sum(v.reshape(-1, 8, 2 * C), axis=0)

    zero8 = jnp.zeros((8, 2 * C), f32)

    def act_of(h):
        return h + h * jnp.tanh(h)

    mean2 = twice(mean[...])
    inv2 = twice(1.0 / std[...])

    def standard(m, q):
        return (XIN[m, q : q + CHUNK].astype(f32) - mean2) * inv2

    def after_conv(b, v, m, r, cots):
        bias = twice(vec(b, 3 * v) * 0.5)
        t0, t1, t2, t3 = zero8, zero8, zero8, zero8
        for q in chunks():
            h = part(r, q) + bias
            HS[b * 2 + v, m, q : q + CHUNK] = h
            act = act_of(h)
            t0, t1 = add8(t0, act), add8(t1, act * act)
            if cots:
                dy = COT[m, q : q + CHUNK].astype(f32)
                t2, t3 = add8(t2, dy), add8(t3, dy * act)
        sums = (fold_rows(t0), fold_rows(t1))
        if cots:
            sums += (fold_rows(t2), fold_rows(t3))
        return sums

    def send_block(src, out, b, t, m, shifted):
        for e in range(2):
            lanes = pl.ds((1 - e) * C, C) if shifted else pl.ds(e * C, C)
            first = e if shifted else 0
            view = src.at[pl.ds(first, Q), :, lanes]
            dst = out.at[sec * half + m, :, e]

            @pl.when(sec == b)
            def _():
                pltpu.make_async_copy(view, dst, olsem.at[t]).start()

            @pl.when(sec != b)
            def _():
                pltpu.make_async_remote_copy(
                    view, dst, ossem.at[t], orsem.at[t], device_id={"section": sib}, device_id_type=MESH
                ).start()

    def wait_blocks(out, b, t):
        many = out.at[pl.ds(0, half)]

        @pl.when(sec == b)
        def _():
            pltpu.make_async_copy(many, many, olsem.at[t]).wait()
            pltpu.make_async_copy(many, many, orsem.at[t]).wait()

        @pl.when(sec != b)
        def _():
            pltpu.make_async_copy(many, many, ossem.at[t]).wait()

    def xc(b, v, m):
        return XC.at[(b * 2 + v) * half + m]

    def slot(stage, m):
        return (stage % 2) * half + m

    def stage0(m, carry):
        both = XIN.at[m]
        pltpu.make_async_copy(both, both, isem.at[m]).wait()
        center = xc(0, 0, m)
        for q in chunks():
            put(center, q, standard(m, q))
        send_sums(slot(0, m), *after_conv(0, 0, m, conv(center, WF.at[0]), False))
        return carry

    def stage_norm1(b, stage, m):
        sc, sh = norm_forward(b, 0, m, take_sums(slot(stage - 1, m)))
        center = xc(b, 1, m)
        for q in chunks():
            put(center, q, act_of(HS[b * 2, m, q : q + CHUNK]) * sc + sh)
        if b == 1:
            both = COT.at[m]
            pltpu.make_async_copy(both, both, isem.at[half + m]).wait()
        send_sums(slot(stage, m), *after_conv(b, 1, m, conv(center, WF.at[b * 2 + 1]), b == 1))

    def stage1(m, carry):
        stage_norm1(0, 1, m)
        return carry

    def stage2(m, carry):
        sc, sh = norm_forward(0, 1, m, take_sums(slot(1, m)))
        center = xc(1, 0, m)
        for q in chunks():
            put(center, q, standard(m, q) + (act_of(HS[1, m, q : q + CHUNK]) * sc + sh))
        send_block(center, bo, 0, 0, m, True)
        send_sums(slot(2, m), *after_conv(1, 0, m, conv(center, WF.at[2]), False))
        return carry

    def stage3(m, carry):
        stage_norm1(1, 3, m)
        return carry

    def back_chunk(i, m, q, dy, coef):
        ca, cb, cc = coef
        h = HS[i, m, q : q + CHUNK]
        u = 1.0 + jnp.tanh(h)
        act = h * u
        dp = (ca * dy + (cc * act + cb)) * (act + (0.5 * u) * (1.0 - act))
        put(LB.at[1], q, dp)
        return act, dp

    def stage_e(b, stage, m):
        total = take_sums(slot(stage - 1, m))
        if b == 1:
            sc, sh = norm_forward(1, 1, m, total)
            coef = norm_backward(1, 1, m, total[2:3], total[3:4])
        else:
            coef = norm_backward(0, 1, m, total[0:1], total[1:2])
            VACC[1, 0:1] += total[2:3]
        t0, t1, t2 = zero8, zero8, zero8
        for q in chunks():
            dy = (COT if b == 1 else DY0)[m, q : q + CHUNK].astype(f32)
            act, dp = back_chunk(b * 2 + 1, m, q, dy, coef)
            t2 = add8(t2, dp)
            if b == 1:
                final = get(xc(1, 0, m), q, CHUNK).astype(f32) + (act * sc + sh)
                XIN[m, q : q + CHUNK] = final.astype(bf16)
        if b == 1:
            send_block(XIN.at[m], bo, 1, 1, m, False)
        r = conv(LB.at[1], WD.at[b * 2 + 1])
        for q in chunks():
            dn = part(r, q)
            DN[m, q : q + CHUNK] = dn
            t0, t1 = add8(t0, dn), add8(t1, dn * act_of(HS[b * 2, m, q : q + CHUNK]))
        send_sums(slot(stage, m), fold_rows(t0), fold_rows(t1), fold_rows(t2))
        wgrad(b * 2 + 1, xc(b, 1, m))

    def stage4(m, carry):
        stage_e(1, 4, m)
        return carry

    def coef_f(b, stage, m):
        total = take_sums(slot(stage - 1, m))
        VACC[b, 3:4] += total[2:3]
        return norm_backward(b, 0, m, total[0:1], total[1:2])

    def low_f(b, m, coef):
        t2 = zero8
        for q in chunks():
            t2 = add8(t2, back_chunk(b * 2, m, q, DN[m, q : q + CHUNK], coef)[1])
        return t2

    def stage5(m, carry):
        t2 = low_f(1, m, coef_f(1, 5, m))
        r = conv(LB.at[1], WD.at[2])
        t0, t1 = zero8, zero8
        for q in chunks():
            da = (COT[m, q : q + CHUNK].astype(f32) + part(r, q)).astype(bf16)
            DY0[m, q : q + CHUNK] = da
            da = da.astype(f32)
            t0, t1 = add8(t0, da), add8(t1, da * act_of(HS[1, m, q : q + CHUNK]))
        send_sums(slot(5, m), fold_rows(t0), fold_rows(t1), fold_rows(t2))
        send_block(DY0.at[m], eg, 1, 2, m, False)
        wgrad(2, xc(1, 0, m))
        return carry

    def taps(b, v):
        a = ACC.at[b * 2 + v]
        for i in range(3):
            for j in range(3):
                out = None
                for t in range(2):
                    for s in range(2):
                        e = 2 * t + s - i
                        if 0 <= e <= 1:
                            r = (2 * t + s) * C
                            c = ((2 - j) * 2 + e) * C
                            d = a[r : r + C, c : c + C]
                            out = d if out is None else out + d
                yield (v * 9 + i * 3 + j) * C, out

    flat = A * PR

    def pieces(row, size):
        while size > 0:
            p, o = row // PR, row % PR
            k = min(size, PR - o)
            yield p // A, p % A, o, k
            row, size = row + k, size - k

    def phase0(b, x):
        for v in range(2):
            for row, val in taps(b, v):
                at = 0
                for pb, pa, o, k in pieces(row, C):
                    GF[pb, pa, o : o + k] = val[at : at + k]
                    at += k

        @pl.when(sec != b)
        def _():
            GS[...] = GF[...].astype(bf16)
            pltpu.make_async_remote_copy(
                GS, GR0, gsend.at[x, 0], grecv.at[x, 0], device_id={"section": sib}, device_id_type=MESH
            ).start()
            pltpu.make_async_copy(GS, GS, gsend.at[x, 0]).wait()

    def phase1(b, x):
        @pl.when(sec == b)
        def _():
            pltpu.make_async_copy(GR0, GR0, grecv.at[x, 0]).wait()
            GF[...] += GR0[...].astype(f32)
            GS[...] = GF[...].astype(bf16)
            GR1[gb] = GS[gb]
            for d in range(1, B):
                to = lax.rem(gb + d, B)
                pltpu.make_async_remote_copy(
                    GS.at[to], GR1.at[gb], gsend.at[x, 1], grecv.at[x, 1],
                    device_id={"dp": ga * B + to}, device_id_type=MESH,
                ).start()

    def group_wait(ref, size, x, p):
        if size > 1:
            many = ref.at[pl.ds(0, size - 1)]
            pltpu.make_async_copy(many, many, grecv.at[x, p]).wait()
            pltpu.make_async_copy(many, many, gsend.at[x, p]).wait()

    def phase2(b, x):
        @pl.when(sec == b)
        def _():
            group_wait(GR1, B, x, 1)
            total = GR1[0].astype(f32)
            for d in range(1, B):
                total = total + GR1[d].astype(f32)
            GQ[...] = total
            GS2[...] = total.astype(bf16)
            GR2[ga] = GS2[ga]
            for d in range(1, A):
                to = lax.rem(ga + d, A)
                pltpu.make_async_remote_copy(
                    GS2.at[to], GR2.at[ga], gsend.at[x, 2], grecv.at[x, 2],
                    device_id={"dp": to * B + gb}, device_id_type=MESH,
                ).start()

    def phase3(b, x):
        @pl.when(sec == b)
        def _():
            group_wait(GR2, A, x, 2)
            total = GR2[0].astype(f32)
            for d in range(1, A):
                total = total + GR2[d].astype(f32)
            GO[gb, ga] = total.astype(bf16)
            for d in range(1, A):
                pltpu.make_async_remote_copy(
                    GO.at[gb, ga], GO.at[gb, ga], gsend.at[x, 3], grecv.at[x, 3],
                    device_id={"dp": lax.rem(ga + d, A) * B + gb}, device_id_type=MESH,
                ).start()

    def phase4(b, x):
        @pl.when(sec == b)
        def _():
            group_wait(GO.at[gb], A, x, 3)
            for d in range(1, B):
                pltpu.make_async_remote_copy(
                    GO.at[gb], GO.at[gb], gsend.at[x, 4], grecv.at[x, 4],
                    device_id={"dp": ga * B + lax.rem(gb + d, B)}, device_id_type=MESH,
                ).start()

    def phase5(b, x):
        @pl.when(sec == b)
        def _():
            group_wait(GO, B, x, 4)
            for v, out in enumerate((gw1, gw2)):
                for k in range(9):
                    at = 0
                    for pb, pa, o, size in pieces((v * 9 + k) * C, C):
                        out[k, at : at + size] = GO[pb, pa, o : o + size].astype(f32)
                        at += size

    @pl.when(sec != 0)
    def _():
        pltpu.make_async_copy(WR.at[0, 0], WR.at[0, 0], wrsem.at[0]).wait()

    prep(0, 0)
    pltpu.make_async_copy(PV.at[0], PV.at[0], wrsem.at[2]).wait()

    @pl.when(sec == 0)
    def _():
        pltpu.make_async_copy(WR.at[0, 0], WR.at[0, 0], wrsem.at[0]).wait()

    lax.fori_loop(0, half, stage0, 0)
    pltpu.make_async_copy(WR.at[0, 1], WR.at[0, 1], wrsem.at[1]).wait()
    for v in range(2):
        pltpu.make_async_copy(WR.at[0, 0], WR.at[0, 0], wssem.at[v]).wait()
    pltpu.make_async_copy(PV.at[0], PV.at[0], wssem.at[2]).wait()
    prep(0, 1)
    lax.fori_loop(0, half, stage1, 0)
    prep(1, 0)
    lax.fori_loop(0, half, stage2, 0)
    prep(1, 1)
    lax.fori_loop(0, half, stage3, 0)
    lax.fori_loop(0, half, stage4, 0)
    lax.fori_loop(0, half, stage5, 0)
    phase0(1, 0)

    def stage6(m, carry):
        stage_e(0, 6, m)

        @pl.when(m == 1)
        def _():
            phase1(1, 0)

        @pl.when(m == half - 1)
        def _():
            phase2(1, 0)

        return carry

    lax.fori_loop(0, half, stage6, 0)

    def stage7(m, carry):
        t2 = low_f(0, m, coef_f(0, 7, m))
        send_sums(slot(7, m), fold_rows(t2))
        wgrad(0, xc(0, 0, m))

        @pl.when(m == 1)
        def _():
            phase3(1, 0)

        @pl.when(m == half - 1)
        def _():
            phase4(1, 0)

        return carry

    lax.fori_loop(0, half, stage7, 0)
    phase0(0, 1)

    def stage8(m, carry):
        mu = ST[0, m, 0:1]
        rstd = ST[0, m, 1:2]
        total = SLOT[slot(6, m), 0]
        for d in range(1, n):
            total = total + SLOT[slot(6, m), d]
        gain_sum = rstd * (total[1:2] - mu * total[0:1])
        ca = vec(0, 1) * rstd
        cc = -ca * rstd * gain_sum / count
        cb = -ca * total[0:1] / count - cc * mu
        low_f(0, m, (twice(ca), twice(cb), twice(cc)))
        r = conv(LB.at[1], WD.at[0])
        for q in chunks():
            da = (DY0[m, q : q + CHUNK].astype(f32) + part(r, q)) * inv2
            COT[m, q : q + CHUNK] = da.astype(bf16)
        send_block(COT.at[m], eg, 0, 3, m, False)

        @pl.when(m == 0)
        def _():
            phase5(1, 0)
            phase1(0, 1)

        @pl.when(m == 2)
        def _():
            phase2(0, 1)

        @pl.when(m == half - 1)
        def _():
            phase3(0, 1)

        return carry

    lax.fori_loop(0, half, stage8, 0)

    for m in range(half):
        VACC[0, 0:1] += take_sums(slot(7, m))[0:1]
    pltpu.make_async_remote_copy(
        VACC.at[sib], VR, vsem.at[0], vsem.at[1], device_id={"section": sib}, device_id_type=MESH
    ).start()
    phase4(0, 1)
    pltpu.make_async_copy(VR, VR, vsem.at[1]).wait()
    pltpu.make_async_copy(VR, VR, vsem.at[0]).wait()
    gvec[...] = VACC[sec] + VR[...]
    phase5(0, 1)
    wait_blocks(bo, 0, 0)
    wait_blocks(bo, 1, 1)
    wait_blocks(eg, 1, 2)
    wait_blocks(eg, 0, 3)


def group_of(n):
    return min(d for d in range(1, n + 1) if n % d == 0 and d * d >= n)


def solution(mesh):
    n = mesh.shape["dp"]
    grp = group_of(n)

    def per_device(inputs, channel_mean, channel_std, cotangent, conv_w1, conv_b1, bn_gain1, bn_shift1, conv_w2, conv_b2, bn_gain2, bn_shift2):
        micro, _, H, W, _ = inputs.shape
        half = micro // 2
        Q = H // 2
        rows = Q * W
        field = (micro, Q, 2, W, C)
        piece = -(-18 * C // n // 16) * 16
        anywhere = pl.BlockSpec(memory_space=pl.ANY)
        vmem = pl.BlockSpec(memory_space=pltpu.VMEM)
        D = pltpu.SemaphoreType.DMA
        V = pltpu.VMEM
        out = pl.pallas_call(
            functools.partial(kernel, n, grp),
            out_shape=[
                jax.ShapeDtypeStruct(field, bf16),
                jax.ShapeDtypeStruct(field, bf16),
                jax.ShapeDtypeStruct((9, C, C), f32),
                jax.ShapeDtypeStruct((9, C, C), f32),
                jax.ShapeDtypeStruct((8, C), f32),
            ],
            in_specs=[anywhere, anywhere, vmem, vmem, anywhere, vmem, vmem, vmem, anywhere, vmem, vmem, vmem],
            out_specs=[anywhere, anywhere, vmem, vmem, vmem],
            scratch_shapes=[
                V((half, Q, W, 2 * C), bf16),
                V((half, Q, W, 2 * C), bf16),
                V((half, Q, W, 2 * C), bf16),
                V((4 * half, Q + 1, W, 2 * C), bf16),
                V((3, Q + 1, W, 2 * C), bf16),
                V((4, half, Q, W, 2 * C), f32),
                V((half, Q, W, 2 * C), f32),
                V((4, 3, 2, 2 * C, 2 * C), bf16),
                V((4, 3, 2, 2 * C, 2 * C), bf16),
                V((4, 4 * C, 6 * C), f32),
                V((2, 2, 9, C, C), bf16),
                V((2, 8, C), f32),
                V((4, half, 8, C), f32),
                V((2, 8, C), f32),
                V((8, C), f32),
                V((2 * half, 4, C), f32),
                V((2 * half, n, 4, C), f32),
                V((grp, n // grp, piece, C), f32),
                V((grp, n // grp, piece, C), bf16),
                V((grp, n // grp, piece, C), bf16),
                V((grp, n // grp, piece, C), bf16),
                V((n // grp, piece, C), f32),
                V((n // grp, piece, C), bf16),
                V((n // grp, piece, C), bf16),
                V((grp, n // grp, piece, C), bf16),
                D((2 * half,)),
                D((2,)),
                D((3,)),
                D((3,)),
                D((2 * half,)),
                D((2 * half,)),
                D((4,)),
                D((4,)),
                D((4,)),
                D((2, 5)),
                D((2, 5)),
                D((2,)),
            ],
            compiler_params=pltpu.CompilerParams(
                collective_id=0, has_side_effects=True, vmem_limit_bytes=62 * 2**20
            ),
        )(
            inputs.reshape(field),
            cotangent.reshape(field),
            channel_mean[None],
            channel_std[None],
            conv_w1.reshape(9, C, C),
            conv_b1,
            bn_gain1,
            bn_shift1,
            conv_w2.reshape(9, C, C),
            conv_b2,
            bn_gain2,
            bn_shift2,
        )
        bo, eg, gw1, gw2, gvec = out
        whole = (1, micro, 1, H, W, C)
        return (
            bo.reshape(whole),
            eg.reshape(whole),
            gw1.reshape(1, 3, 3, C, C),
            gvec[0:1],
            gvec[1:2],
            gvec[2:3],
            gw2.reshape(1, 3, 3, C, C),
            gvec[3:4],
            gvec[4:5],
            gvec[5:6],
        )

    in_specs = (
        P(None, "dp", None, None, None),
        P(),
        P(),
        P(None, "dp", None, None, None),
        P("section", None, None, None, None),
        P("section", None),
        P("section", None),
        P("section", None),
        P("section", None, None, None, None),
        P("section", None),
        P("section", None),
        P("section", None),
    )
    out_specs = (
        P("section", None, "dp", None, None, None),
        P("section", None, "dp", None, None, None),
        P("section", None, None, None, None),
        P("section", None),
        P("section", None),
        P("section", None),
        P("section", None, None, None, None),
        P("section", None),
        P("section", None),
        P("section", None),
    )
    return jax.shard_map(per_device, mesh=mesh, in_specs=in_specs, out_specs=out_specs, check_vma=False)
```

```python
import functools

import jax
import jax.numpy as jnp
from jax import lax
from jax.experimental import pallas as pl
from jax.experimental.pallas import tpu as pltpu
from jax.sharding import PartitionSpec as P

norm_eps = 1e-05
MESH = pl.DeviceIdType.MESH
bf16 = jnp.bfloat16
f32 = jnp.float32
C = 128
CHUNK = 2
VMEM_LIMIT = 52 * 2**20


def dot(a, b):
    return jnp.dot(a, b, preferred_element_type=f32)


def twice(v):
    return jnp.concatenate([v, v], axis=-1)


def fold_rows(v):
    one = jnp.sum(v, axis=0, keepdims=True)
    return one[:, :C] + one[:, C:]


def piece_rows(rows, n):
    size = -(-rows // n // 16) * 16
    return size, -(-rows // size)


def kernel(n, *refs):
    (
        inp, cot, mean, std, w1, b1, g1, s1, w2, b2, g2, s2,
        bo, eg, GO2, GO1, gvec,
        XIN, COT, XC, LB, HS, WF, WD, ACC, WR, PV, ST, VACC, VR,
        MSG, SLOT, GS2, GS1, GR2, GR1, GP2, GP1,
        isem, wlsem, wssem, wrsem, msend, mrecv, olsem, ossem, orsem, gsend, grecv, vsem,
    ) = refs
    micro = inp.shape[0]
    half = micro // 2
    Q = inp.shape[1]
    W = inp.shape[3]
    rows = Q * W
    count = float(2 * rows * n)

    me = lax.axis_index("dp")
    sec = lax.axis_index("section")
    sib = 1 - sec

    def peer(d):
        return {"dp": lax.rem(me + d, n)}

    def every_peer(body):
        if n <= 16:
            for d in range(1, n):
                body(d)
        else:
            lax.fori_loop(1, n, lambda d, carry: (body(d), carry)[1], 0)

    def wait(ref, sem):
        pltpu.make_async_copy(ref, ref, sem).wait()

    def to_sibling(src, dst, send, recv):
        pltpu.make_async_remote_copy(
            src, dst, send, recv, device_id={"section": sib}, device_id_type=MESH
        ).start()

    barrier = pltpu.get_barrier_semaphore()
    pl.semaphore_signal(barrier, inc=1, device_id={"section": sib}, device_id_type=MESH)
    every_peer(lambda d: pl.semaphore_signal(barrier, inc=1, device_id=peer(d), device_id_type=MESH))

    for v, ref in enumerate((w1, w2)):
        pltpu.make_async_copy(ref, WR.at[sec, v], wlsem.at[v]).start()
    for src, dst, at in ((inp, XIN, 0), (cot, COT, half)):
        for m in range(half):
            for e in range(2):
                pltpu.make_async_copy(
                    src.at[sec * half + m, :, e], dst.at[m, :, :, pl.ds(e * C, C)], isem.at[at + m]
                ).start()

    for v, ref in enumerate((b1, g1, s1, b2, g2, s2)):
        PV[sec, v : v + 1] = ref[...]

    halo = jnp.zeros((W, C), bf16)
    for j in range(2):
        LB[j, 0, :, 0:C] = halo
        LB[j, Q, :, C : 2 * C] = halo

    def zero_halo(i, carry):
        XC[i, 0, :, 0:C] = halo
        XC[i, Q, :, C : 2 * C] = halo
        return carry

    lax.fori_loop(0, 4 * half + 1, zero_halo, 0)
    empty = jnp.zeros((C, C), bf16)
    for i in range(4):
        ACC[i] = jnp.zeros(ACC.shape[1:], f32)
        for j in range(3):
            for ref in (WF, WD):
                ref[i, j, 0, 0:C, C : 2 * C] = empty
                ref[i, j, 1, C : 2 * C, 0:C] = empty
    VACC[...] = jnp.zeros(VACC.shape, f32)
    GS2[...] = jnp.zeros(GS2.shape, bf16)
    GS1[...] = jnp.zeros(GS1.shape, bf16)

    pl.semaphore_wait(barrier, n)

    to_sibling(PV.at[sec], PV.at[sec], wssem.at[2], wrsem.at[2])
    for v in range(2):
        wait(WR.at[sec, v], wlsem.at[v])
        to_sibling(WR.at[sec, v], WR.at[sec, v], wssem.at[v], wrsem.at[v])

    def blocks():
        for j in range(3):
            for t in range(2):
                for s in range(2):
                    for e in range(2):
                        i = 2 * t + s - e
                        if 0 <= i <= 2:
                            yield i, j, t, slice(s * C, s * C + C), slice(e * C, e * C + C)

    def prep_forward(b, v):
        for i, j, t, r, c in blocks():
            WF[b * 2 + v, j, t, r, c] = (WR[b, v, i * 3 + j].astype(f32) * 0.5).astype(bf16)

    def prep_backward(b, v):
        for i, j, t, r, c in blocks():
            WD[b * 2 + v, j, t, r, c] = WR[b, v, (2 - i) * 3 + 2 - j].T

    def vec(b, v):
        return PV[b, v : v + 1]

    def send_sums(i, *sums):
        for r, v in enumerate(sums):
            MSG[i, r : r + 1] = v
        SLOT[i, me] = MSG[i]
        every_peer(
            lambda d: pltpu.make_async_remote_copy(
                MSG.at[i], SLOT.at[i, me], msend.at[i], mrecv.at[i], device_id=peer(d), device_id_type=MESH
            ).start()
        )

    def sum_slots(i):
        total = SLOT[i, 0]
        for d in range(1, n):
            total = total + SLOT[i, d]
        return total

    def take_sums(i):
        if n > 1:
            many = SLOT.at[i, pl.ds(0, n - 1)]
            wait(many, mrecv.at[i])
            wait(many, msend.at[i])
        return sum_slots(i)

    def norm_forward(b, v, m, total):
        mu = total[0:1] / count
        rstd = lax.rsqrt(total[1:2] / count - mu * mu + norm_eps)
        ST[b * 2 + v, m, 0:1] = mu
        ST[b * 2 + v, m, 1:2] = rstd
        sc = vec(b, 1 + 3 * v) * rstd
        return twice(sc), twice(vec(b, 2 + 3 * v) - mu * sc)

    def norm_backward(b, v, m, shift_sum, prod_sum):
        mu = ST[b * 2 + v, m, 0:1]
        rstd = ST[b * 2 + v, m, 1:2]
        gain_sum = rstd * (prod_sum - mu * shift_sum)
        VACC[b, 3 * v + 1 : 3 * v + 2] += gain_sum
        VACC[b, 3 * v + 2 : 3 * v + 3] += shift_sum
        ca = vec(b, 1 + 3 * v) * rstd
        cc = -ca * rstd * gain_sum / count
        cb = -ca * shift_sum / count - cc * mu
        return twice(ca), twice(cb), twice(cc)

    def put(trio, q, v):
        k = v.shape[0]
        for j, ref in enumerate(trio):
            u = (v if j == 1 else pltpu.roll(v, 1 if j == 0 else W - 1, 1)).astype(bf16)
            ref[q : q + k, :, C : 2 * C] = u[:, :, :C]
            ref[q + 1 : q + k + 1, :, 0:C] = u[:, :, C:]

    def get(center, q, k):
        return jnp.concatenate([center[q : q + k, :, C : 2 * C], center[q + 1 : q + k + 1, :, 0:C]], axis=-1)

    def conv(trio, w):
        acc = None
        for j, ref in enumerate(trio):
            for t in range(2):
                d = dot(ref[t : t + Q].reshape(rows, 2 * C), w[j, t])
                acc = d if acc is None else acc + d
        return acc

    def wgrad(i, center, trio, which=(0, 1, 2)):
        left = jnp.concatenate([center[0:Q].reshape(rows, 2 * C), center[1 : Q + 1].reshape(rows, 2 * C)], axis=-1)
        for j in which:
            right = get(trio[j], 0, Q).reshape(rows, 2 * C)
            ACC[i, :, j * 2 * C : (j + 1) * 2 * C] += lax.dot_general(
                left, right, (((0,), (0,)), ((), ())), preferred_element_type=f32
            )

    def chunks():
        return range(0, Q, CHUNK)

    def part(r, q):
        return r[q * W : (q + CHUNK) * W].reshape(CHUNK, W, 2 * C)

    def add8(total, v):
        return total + jnp.sum(v.reshape(-1, 8, 2 * C), axis=0)

    zero8 = jnp.zeros((8, 2 * C), f32)

    def act_of(h):
        return h + h * jnp.tanh(h)

    mean2 = twice(mean[...])
    inv2 = twice(1.0 / std[...])

    def standard(m, q):
        return (XIN[m, q : q + CHUNK].astype(f32) - mean2) * inv2

    def after_conv(b, v, m, r, cots):
        bias = twice(vec(b, 3 * v) * 0.5)
        t0, t1, t2, t3 = zero8, zero8, zero8, zero8
        for q in chunks():
            h = part(r, q) + bias
            HS[b * 2 + v, m, q : q + CHUNK] = h
            act = act_of(h)
            t0, t1 = add8(t0, act), add8(t1, act * act)
            if cots:
                dy = COT[m, q : q + CHUNK].astype(f32)
                t2, t3 = add8(t2, dy), add8(t3, dy * act)
        sums = (fold_rows(t0), fold_rows(t1))
        if cots:
            sums += (fold_rows(t2), fold_rows(t3))
        return sums

    def send_block(views, b, t):
        @pl.when(sec == b)
        def _():
            for src, dst in views:
                pltpu.make_async_copy(src, dst, olsem.at[t]).start()

        @pl.when(sec != b)
        def _():
            for src, dst in views:
                to_sibling(src, dst, ossem.at[t], orsem.at[t])

    def sent_blocks(out, b, t):
        many = out.at[pl.ds(0, half)]

        @pl.when(sec == b)
        def _():
            wait(many, olsem.at[t])

        @pl.when(sec != b)
        def _():
            wait(many, ossem.at[t])

    def came_blocks(out, b, t):
        @pl.when(sec == b)
        def _():
            wait(out.at[pl.ds(0, half)], orsem.at[t])

    def xc(b, v, m):
        return XC.at[(b * 2 + v) * half + m]

    def trio_of(center):
        return LB.at[0], center, LB.at[1]

    low = trio_of(XC.at[4 * half])

    def slot(stage, m):
        return (stage % 2) * half + m

    def stage0(m, carry):
        wait(XIN.at[m], isem.at[m])
        trio = trio_of(xc(0, 0, m))
        for q in chunks():
            put(trio, q, standard(m, q))
        send_sums(slot(0, m), *after_conv(0, 0, m, conv(trio, WF.at[0]), False))
        return carry

    def stage_norm1(b, stage, m):
        sc, sh = norm_forward(b, 0, m, take_sums(slot(stage - 1, m)))
        if b == 1:
            wait(COT.at[m], isem.at[half + m])
        trio = trio_of(xc(b, 1, m))
        for q in chunks():
            put(trio, q, act_of(HS[b * 2, m, q : q + CHUNK]) * sc + sh)
        send_sums(slot(stage, m), *after_conv(b, 1, m, conv(trio, WF.at[b * 2 + 1]), b == 1))

    def stage1(m, carry):
        stage_norm1(0, 1, m)
        return carry

    def stage2(m, carry):
        sc, sh = norm_forward(0, 1, m, take_sums(slot(1, m)))
        center = xc(1, 0, m)
        trio = trio_of(center)
        for q in chunks():
            put(trio, q, standard(m, q) + (act_of(HS[1, m, q : q + CHUNK]) * sc + sh))
        send_sums(slot(2, m), *after_conv(1, 0, m, conv(trio, WF.at[2]), False))
        send_block(
            [
                (center.at[pl.ds(e, Q), :, pl.ds((1 - e) * C, C)], bo.at[sec * half + m, :, :, pl.ds(e * C, C)])
                for e in range(2)
            ],
            0,
            0,
        )
        return carry

    def stage3(m, carry):
        stage_norm1(1, 3, m)
        return carry

    def back_chunk(trio, i, m, q, dy, coef):
        ca, cb, cc = coef
        h = HS[i, m, q : q + CHUNK]
        u = 1.0 + jnp.tanh(h)
        act = h * u
        dp = (ca * dy + (cc * act + cb)) * (act + (0.5 * u) * (1.0 - act))
        put(trio, q, dp)
        return act, dp

    def stage_e(b, stage, m):
        total = take_sums(slot(stage - 1, m))
        if b == 1:
            sc, sh = norm_forward(1, 1, m, total)
            coef = norm_backward(1, 1, m, total[2:3], total[3:4])
        else:
            coef = norm_backward(0, 1, m, total[0:1], total[1:2])
            VACC[1, 0:1] += total[2:3]
        t0, t1, t2 = zero8, zero8, zero8
        i = b * 2 + 1
        for q in chunks():
            dy = COT[m, q : q + CHUNK].astype(f32)
            act, dp = back_chunk(low, i, m, q, dy, coef)
            t2 = add8(t2, dp)
            if b == 1:
                final = get(xc(1, 0, m), q, CHUNK).astype(f32) + (act * sc + sh)
                XIN[m, q : q + CHUNK] = final.astype(bf16)
        r = conv(low, WD.at[i])
        wgrad(i, xc(b, 1, m), low)
        for q in chunks():
            dn = part(r, q)
            HS[i, m, q : q + CHUNK] = dn
            t0, t1 = add8(t0, dn), add8(t1, dn * act_of(HS[b * 2, m, q : q + CHUNK]))
        send_sums(slot(stage, m), fold_rows(t0), fold_rows(t1), fold_rows(t2))
        if b == 1:
            send_block([(XIN.at[m], bo.at[sec * half + m])], 1, 1)

    def stage4(m, carry):
        stage_e(1, 4, m)
        return carry

    def coef_f(b, stage, m):
        total = take_sums(slot(stage - 1, m))
        VACC[b, 3:4] += total[2:3]
        return norm_backward(b, 0, m, total[0:1], total[1:2])

    def low_f(trio, b, m, coef):
        t2 = zero8
        for q in chunks():
            t2 = add8(t2, back_chunk(trio, b * 2, m, q, HS[b * 2 + 1, m, q : q + CHUNK], coef)[1])
        return t2

    def stage5(m, carry):
        t2 = low_f(low, 1, m, coef_f(1, 5, m))
        r = conv(low, WD.at[2])
        wgrad(2, xc(1, 0, m), low)
        t0, t1 = zero8, zero8
        for q in chunks():
            da = (COT[m, q : q + CHUNK].astype(f32) + part(r, q)).astype(bf16)
            COT[m, q : q + CHUNK] = da
            da = da.astype(f32)
            t0, t1 = add8(t0, da), add8(t1, da * act_of(HS[1, m, q : q + CHUNK]))
        send_sums(slot(5, m), fold_rows(t0), fold_rows(t1), fold_rows(t2))
        send_block([(COT.at[m], eg.at[sec * half + m])], 1, 2)

        @pl.when(m == 1)
        def _():
            to_owners(1, 0)

        return carry

    def buffers(x):
        if x == 0:
            return GS2, GR2, GP2, GO2
        return GS1.at[x - 1], GR1.at[x - 1], GP1.at[x - 1], GO1.at[x - 1]

    def taps(b, x):
        a = ACC.at[b * 2 + (1 if x == 0 else 0)]
        for i in range(3):
            for j in range(3) if x == 0 else (x - 1,):
                out = None
                for t in range(2):
                    for s in range(2):
                        e = 2 * t + s - i
                        if 0 <= e <= 1:
                            r = (2 * t + s) * C
                            c = ((2 - j) * 2 + e) * C
                            d = a[r : r + C, c : c + C]
                            out = d if out is None else out + d
                yield (i * 3 + j if x == 0 else i) * C, out

    def to_pair(b, x):
        gs, gr, _, _ = buffers(x)

        @pl.when(sec != b)
        def _():
            for row, val in taps(b, x):
                gs[row : row + C] = val.astype(bf16)
            to_sibling(gs, gr, gsend.at[x, 0], grecv.at[x, 0])

    def piece(ref, x, p):
        size = GP2.shape[1] if x == 0 else GP1.shape[2]
        return ref.at[pl.ds(pl.multiple_of(p * size, 16), size)]

    def span(ref, x, k):
        size = GP2.shape[1] if x == 0 else GP1.shape[2]
        return ref.at[pl.ds(0, k * size)]

    def owners(x):
        return (GO2.shape[0] // GP2.shape[1]) if x == 0 else (GO1.shape[1] // GP1.shape[2])

    def when_owner(x, p, body):
        if owners(x) == n:
            body()
        else:
            pl.when(p < owners(x))(body)

    def to_owners(b, x):
        gs, gr, gp, _ = buffers(x)

        @pl.when(sec == b)
        def _():
            wait(gr, grecv.at[x, 0])
            for row, val in taps(b, x):
                gs[row : row + C] = (val + gr[row : row + C].astype(f32)).astype(bf16)

            def keep():
                gp[me] = piece(gs, x, me)[...]

            when_owner(x, me, keep)

            def one(d):
                to = lax.rem(me + d, n)

                def go():
                    pltpu.make_async_remote_copy(
                        piece(gs, x, to), gp.at[me], gsend.at[x, 1], grecv.at[x, 1],
                        device_id={"dp": to}, device_id_type=MESH,
                    ).start()

                when_owner(x, to, go)

            every_peer(one)

    def to_all(b, x):
        gs, _, gp, go = buffers(x)
        k = owners(x)

        @pl.when(sec == b)
        def _():
            def mine():
                if n > 1:
                    wait(gp.at[pl.ds(0, n - 1)], grecv.at[x, 1])
                if k > 1:
                    wait(span(gs, x, k - 1), gsend.at[x, 1])
                total = gp[0].astype(f32)
                for d in range(1, n):
                    total = total + gp[d].astype(f32)
                piece(go, x, me)[...] = total.astype(bf16)
                every_peer(
                    lambda d: pltpu.make_async_remote_copy(
                        piece(go, x, me), piece(go, x, me), gsend.at[x, 2], grecv.at[x, 2],
                        device_id=peer(d), device_id_type=MESH,
                    ).start()
                )

            when_owner(x, me, mine)
            if k < n:
                @pl.when(me >= k)
                def _():
                    wait(span(gs, x, k), gsend.at[x, 1])

    def finish(b, x):
        gs, _, gp, go = buffers(x)
        k = owners(x)

        @pl.when(sec == b)
        def _():
            def mine():
                if k > 1:
                    wait(span(go, x, k - 1), grecv.at[x, 2])
                if n > 1:
                    wait(gp.at[pl.ds(0, n - 1)], gsend.at[x, 2])

            when_owner(x, me, mine)
            if k < n:
                @pl.when(me >= k)
                def _():
                    wait(span(go, x, k), grecv.at[x, 2])

        @pl.when(sec != b)
        def _():
            wait(gs, gsend.at[x, 0])

    @pl.when(sec != 0)
    def _():
        wait(WR.at[0, 0], wrsem.at[0])

    prep_forward(0, 0)
    wait(PV.at[0], wrsem.at[2])
    lax.fori_loop(0, half, stage0, 0)

    @pl.when(sec == 0)
    def _():
        wait(WR.at[0, 0], wrsem.at[0])

    wait(WR.at[0, 1], wrsem.at[1])
    for v in range(2):
        wait(WR.at[0, 0], wssem.at[v])
    wait(PV.at[0], wssem.at[2])
    prep_forward(0, 1)
    prep_backward(0, 0)
    lax.fori_loop(0, half, stage1, 0)
    prep_forward(1, 0)
    prep_backward(0, 1)
    lax.fori_loop(0, half, stage2, 0)
    prep_forward(1, 1)
    prep_backward(1, 1)
    lax.fori_loop(0, half, stage3, 0)
    prep_backward(1, 0)
    lax.fori_loop(0, half, stage4, 0)
    to_pair(1, 0)
    lax.fori_loop(0, half, stage5, 0)
    for x in range(1, 4):
        to_pair(1, x)

    def stage6(m, carry):
        stage_e(0, 6, m)

        @pl.when(m == 1)
        def _():
            for x in range(1, 4):
                to_owners(1, x)

        @pl.when(m == 2)
        def _():
            to_all(1, 0)

        return carry

    lax.fori_loop(0, half, stage6, 0)
    finish(1, 0)
    to_pair(0, 0)
    sent_blocks(bo, 0, 0)

    def last_trio(m):
        return xc(1, 1, m), xc(0, 1, m), xc(1, 0, m)

    def stage7(m, carry):
        t2 = low_f(last_trio(m), 0, m, coef_f(0, 7, m))
        wgrad(0, xc(0, 0, m), last_trio(m), (2,))
        send_sums(slot(7, m), fold_rows(t2))

        @pl.when(m == 1)
        def _():
            for x in range(1, 4):
                to_all(1, x)

        @pl.when(m == half - 1)
        def _():
            for x in range(1, 4):
                finish(1, x)

        return carry

    lax.fori_loop(0, half, stage7, 0)
    to_pair(0, 1)

    def stage7b(m, carry):
        wgrad(0, xc(0, 0, m), last_trio(m), (1,))
        return carry

    lax.fori_loop(0, half, stage7b, 0)
    to_pair(0, 2)
    to_owners(0, 0)
    to_owners(0, 1)

    def stage7c(m, carry):
        wgrad(0, xc(0, 0, m), last_trio(m), (0,))
        return carry

    lax.fori_loop(0, half, stage7c, 0)
    to_pair(0, 3)
    to_owners(0, 2)
    sent_blocks(eg, 1, 2)

    def stage8(m, carry):
        r = conv(last_trio(m), WD.at[0])
        for q in chunks():
            da = (COT[m, q : q + CHUNK].astype(f32) + part(r, q)) * inv2
            COT[m, q : q + CHUNK] = da.astype(bf16)
        send_block([(COT.at[m], eg.at[sec * half + m])], 0, 3)

        @pl.when(m == 0)
        def _():
            to_owners(0, 3)

        @pl.when(m == half - 1)
        def _():
            to_all(0, 1)

        return carry

    lax.fori_loop(0, half, stage8, 0)

    for m in range(half):
        VACC[0, 0:1] += take_sums(slot(7, m))[0:1]
    to_sibling(VACC.at[sib], VR, vsem.at[0], vsem.at[1])
    to_all(0, 0)
    to_all(0, 2)
    to_all(0, 3)
    wait(VR, vsem.at[1])
    wait(VR, vsem.at[0])
    gvec[...] = VACC[sec] + VR[...]
    sent_blocks(bo, 1, 1)
    sent_blocks(eg, 0, 3)
    came_blocks(bo, 0, 0)
    came_blocks(bo, 1, 1)
    came_blocks(eg, 1, 2)
    came_blocks(eg, 0, 3)
    for x in (0, 1, 2, 3):
        finish(0, x)


def writer(*refs):
    bo_in, eg_in, go2, go1, gvec, bo, eg, gw1, gw2 = refs[:9]
    vecs, sem = refs[9:15], refs[15]
    copies = []
    for k, (src, dst) in enumerate(((bo_in, bo), (eg_in, eg))):
        for m in range(src.shape[0]):
            for e in range(2):
                copies.append(
                    pltpu.make_async_copy(src.at[m, :, :, pl.ds(e * C, C)], dst.at[m, :, e], sem.at[k, m, e])
                )
                copies[-1].start()
    for k in range(9):
        gw2[k] = go2[k * C : (k + 1) * C].astype(f32)
        gw1[k] = go1[k % 3, k // 3 * C : (k // 3 + 1) * C].astype(f32)
    for k, ref in enumerate(vecs):
        ref[...] = gvec[k : k + 1]
    for copy in copies:
        copy.wait()


def solution(mesh):
    n = mesh.shape["dp"]
    size2, own2 = piece_rows(9 * C, n)
    size1, own1 = piece_rows(3 * C, n)

    def per_device(inputs, channel_mean, channel_std, cotangent, conv_w1, conv_b1, bn_gain1, bn_shift1, conv_w2, conv_b2, bn_gain2, bn_shift2):
        micro, _, H, W, _ = inputs.shape
        half = micro // 2
        Q = H // 2
        field = (micro, Q, 2, W, C)
        pairs = (micro, Q, W, 2 * C)
        anywhere = pl.BlockSpec(memory_space=pl.ANY)
        vmem = pl.BlockSpec(memory_space=pltpu.VMEM)
        D = pltpu.SemaphoreType.DMA
        V = pltpu.VMEM
        mid = pl.pallas_call(
            functools.partial(kernel, n),
            out_shape=[
                V(pairs, bf16),
                V(pairs, bf16),
                V((own2 * size2, C), bf16),
                V((3, own1 * size1, C), bf16),
                V((8, C), f32),
            ],
            in_specs=[anywhere, anywhere, vmem, vmem, anywhere, vmem, vmem, vmem, anywhere, vmem, vmem, vmem],
            out_specs=[vmem] * 5,
            scratch_shapes=[
                V((half, Q, W, 2 * C), bf16),
                V((half, Q, W, 2 * C), bf16),
                V((4 * half + 1, Q + 1, W, 2 * C), bf16),
                V((2, Q + 1, W, 2 * C), bf16),
                V((4, half, Q, W, 2 * C), f32),
                V((4, 3, 2, 2 * C, 2 * C), bf16),
                V((4, 3, 2, 2 * C, 2 * C), bf16),
                V((4, 4 * C, 6 * C), f32),
                V((2, 2, 9, C, C), bf16),
                V((2, 8, C), f32),
                V((4, half, 8, C), f32),
                V((2, 8, C), f32),
                V((8, C), f32),
                V((2 * half, 4, C), f32),
                V((2 * half, n, 4, C), f32),
                V((own2 * size2, C), bf16),
                V((3, own1 * size1, C), bf16),
                V((own2 * size2, C), bf16),
                V((3, own1 * size1, C), bf16),
                V((n, size2, C), bf16),
                V((3, n, size1, C), bf16),
                D((2 * half,)),
                D((2,)),
                D((3,)),
                D((3,)),
                D((2 * half,)),
                D((2 * half,)),
                D((4,)),
                D((4,)),
                D((4,)),
                D((4, 3)),
                D((4, 3)),
                D((2,)),
            ],
            compiler_params=pltpu.CompilerParams(
                collective_id=0, has_side_effects=True, vmem_limit_bytes=VMEM_LIMIT
            ),
        )(
            inputs.reshape(field),
            cotangent.reshape(field),
            channel_mean[None],
            channel_std[None],
            conv_w1.reshape(9, C, C),
            conv_b1,
            bn_gain1,
            bn_shift1,
            conv_w2.reshape(9, C, C),
            conv_b2,
            bn_gain2,
            bn_shift2,
        )
        bo, eg, gw1, gw2, *vecs = pl.pallas_call(
            writer,
            out_shape=[
                jax.ShapeDtypeStruct(field, bf16),
                jax.ShapeDtypeStruct(field, bf16),
                jax.ShapeDtypeStruct((9, C, C), f32),
                jax.ShapeDtypeStruct((9, C, C), f32),
            ]
            + [jax.ShapeDtypeStruct((1, C), f32)] * 6,
            in_specs=[vmem] * 5,
            out_specs=[anywhere, anywhere] + [vmem] * 8,
            scratch_shapes=[D((2, micro, 2))],
        )(*mid)
        whole = (1, micro, 1, H, W, C)
        kernel_shape = (1, 3, 3, C, C)
        return (
            bo.reshape(whole),
            eg.reshape(whole),
            gw1.reshape(kernel_shape),
            vecs[0],
            vecs[1],
            vecs[2],
            gw2.reshape(kernel_shape),
            vecs[3],
            vecs[4],
            vecs[5],
        )

    in_specs = (
        P(None, "dp", None, None, None),
        P(),
        P(),
        P(None, "dp", None, None, None),
        P("section", None, None, None, None),
        P("section", None),
        P("section", None),
        P("section", None),
        P("section", None, None, None, None),
        P("section", None),
        P("section", None),
        P("section", None),
    )
    out_specs = (
        P("section", None, "dp", None, None, None),
        P("section", None, "dp", None, None, None),
        P("section", None, None, None, None),
        P("section", None),
        P("section", None),
        P("section", None),
        P("section", None, None, None, None),
        P("section", None),
        P("section", None),
        P("section", None),
    )
    return jax.shard_map(per_device, mesh=mesh, in_specs=in_specs, out_specs=out_specs, check_vma=False)
```

```python
import functools

import jax
import jax.numpy as jnp
from jax import lax
from jax.experimental import pallas as pl
from jax.experimental.pallas import tpu as pltpu
from jax.sharding import PartitionSpec as P

norm_eps = 1e-05
MESH = pl.DeviceIdType.MESH
bf16 = jnp.bfloat16
f32 = jnp.float32
C = 128
VMEM_LIMIT = 55 * 2**20


def dot(a, b):
    return jnp.dot(a, b, preferred_element_type=f32)


def fold_rows(v):
    return jnp.sum(v, axis=0, keepdims=True)


def piece_rows(rows, n):
    size = -(-rows // max(1, n // 2) // 16) * 16
    return size, -(-rows // size)


def kernel(n, *refs):
    (
        inp, cot, mean, std, w1, b1, g1, s1, w2, b2, g2, s2,
        bo, eg, GO2, GO1, gvec,
        XIN, COT, XC, LOW0, LOW1, HS, WF, WD, ACC, WR, PV, ST, VACC, VR,
        MSG, SLOT, PS2, PS1, GS2, GS1, GR2, GR1, GP2, GP1,
        isem, wlsem, wssem, wrsem, msend, mrecv, olsem, ossem, orsem, gsend, grecv, vsem,
    ) = refs
    micro = inp.shape[0]
    half = micro // 2
    Q = inp.shape[1]
    W = inp.shape[3]
    rows = Q * W
    count = float(2 * rows * n)

    me = lax.axis_index("dp")
    sec = lax.axis_index("section")
    sib = 1 - sec

    def peer(d):
        return {"dp": lax.rem(me + d, n)}

    def every_peer(body):
        if n <= 16:
            for d in range(1, n):
                body(d)
        else:
            lax.fori_loop(1, n, lambda d, carry: (body(d), carry)[1], 0)

    def wait(ref, sem):
        pltpu.make_async_copy(ref, ref, sem).wait()

    def to_sibling(src, dst, send, recv):
        pltpu.make_async_remote_copy(
            src, dst, send, recv, device_id={"section": sib}, device_id_type=MESH
        ).start()

    barrier = pltpu.get_barrier_semaphore()
    pl.semaphore_signal(barrier, inc=1, device_id={"section": sib}, device_id_type=MESH)
    every_peer(lambda d: pl.semaphore_signal(barrier, inc=1, device_id=peer(d), device_id_type=MESH))

    for v, ref in enumerate((w1, w2)):
        pltpu.make_async_copy(ref, WR.at[sec, v], wlsem.at[v]).start()
    for src, dst, at in ((inp, XIN, 0), (cot, COT, half)):
        for m in range(half):
            for e in range(2):
                pltpu.make_async_copy(
                    src.at[sec * half + m, :, e], dst.at[m, :, :, pl.ds(e * C, C)], isem.at[at + m]
                ).start()

    for v, ref in enumerate((b1, g1, s1, b2, g2, s2)):
        PV[sec, v : v + 1] = ref[...]

    halo = jnp.zeros((W, C), bf16)
    for j in range(3):
        LOW0[j, 0, :, 0:C] = halo
        LOW0[j, Q, :, C : 2 * C] = halo
    LOW1[...] = jnp.zeros(LOW1.shape, bf16)

    def zero_halo(i, carry):
        XC[i, 0, :, 0:C] = halo
        XC[i, Q, :, C : 2 * C] = halo
        return carry

    lax.fori_loop(0, 4 * half, zero_halo, 0)
    empty = jnp.zeros((C, C), bf16)
    for i in range(4):
        ACC[i] = jnp.zeros(ACC.shape[1:], f32)
        for j in range(3):
            for ref in (WF, WD):
                ref[i, j, 0, 0:C, C : 2 * C] = empty
                ref[i, j, 1, C : 2 * C, 0:C] = empty
    VACC[...] = jnp.zeros(VACC.shape, f32)
    for ref in (PS2, PS1, GS2, GS1):
        ref[...] = jnp.zeros(ref.shape, bf16)

    pl.semaphore_wait(barrier, n)

    to_sibling(PV.at[sec], PV.at[sec], wssem.at[2], wrsem.at[2])
    for v in range(2):
        wait(WR.at[sec, v], wlsem.at[v])
        to_sibling(WR.at[sec, v], WR.at[sec, v], wssem.at[v], wrsem.at[v])

    def blocks():
        for j in range(3):
            for t in range(2):
                for s in range(2):
                    for e in range(2):
                        i = 2 * t + s - e
                        if 0 <= i <= 2:
                            yield i, j, t, slice(s * C, s * C + C), slice(e * C, e * C + C)

    def prep_forward(b, v):
        for i, j, t, r, c in blocks():
            WF[b * 2 + v, j, t, r, c] = (WR[b, v, i * 3 + j].astype(f32) * 0.5).astype(bf16)

    def prep_backward(b, v):
        for i, j, t, r, c in blocks():
            WD[b * 2 + v, j, t, r, c] = WR[b, v, (2 - i) * 3 + 2 - j].T

    def vec(b, v):
        return PV[b, v : v + 1]

    def send_sums(i, *sums):
        for r, v in enumerate(sums):
            MSG[i, r : r + 1] = v
        SLOT[i, me] = MSG[i]
        every_peer(
            lambda d: pltpu.make_async_remote_copy(
                MSG.at[i], SLOT.at[i, me], msend.at[i], mrecv.at[i], device_id=peer(d), device_id_type=MESH
            ).start()
        )

    def sum_slots(i):
        total = SLOT[i, 0]
        for d in range(1, n):
            total = total + SLOT[i, d]
        return total

    def take_sums(i):
        if n > 1:
            many = SLOT.at[i, pl.ds(0, n - 1)]
            wait(many, mrecv.at[i])
            wait(many, msend.at[i])
        return sum_slots(i)

    def norm_forward(b, v, m, total):
        mu = total[0:1] / count
        rstd = lax.rsqrt(total[1:2] / count - mu * mu + norm_eps)
        ST[b * 2 + v, m, 0:1] = mu
        ST[b * 2 + v, m, 1:2] = rstd
        sc = vec(b, 1 + 3 * v) * rstd
        return sc, vec(b, 2 + 3 * v) - mu * sc

    def norm_backward(b, v, m, shift_sum, prod_sum):
        mu = ST[b * 2 + v, m, 0:1]
        rstd = ST[b * 2 + v, m, 1:2]
        gain_sum = rstd * (prod_sum - mu * shift_sum)
        VACC[b, 3 * v + 1 : 3 * v + 2] += gain_sum
        VACC[b, 3 * v + 2 : 3 * v + 3] += shift_sum
        ca = vec(b, 1 + 3 * v) * rstd
        cc = -ca * rstd * gain_sum / count
        cb = -ca * shift_sum / count - cc * mu
        return ca, cb, cc

    def spot(q, e):
        return q + e, slice(None), slice((1 - e) * C, (2 - e) * C)

    def put(trio, q, e, v):
        for j, ref in enumerate(trio):
            ref[spot(q, e)] = (v if j == 1 else pltpu.roll(v, 1 if j == 0 else W - 1, 0)).astype(bf16)

    def get_all(center):
        both = [center[0:Q, :, C : 2 * C], center[1 : Q + 1, :, 0:C]]
        return jnp.concatenate(both, axis=-1).reshape(rows, 2 * C)

    def conv(trio, w):
        acc = None
        for j, ref in enumerate(trio):
            for t in range(2):
                d = dot(ref[t : t + Q].reshape(rows, 2 * C), w[j, t])
                acc = d if acc is None else acc + d
        return acc

    def wgrad(i, center, trio, which=(0, 1, 2)):
        left = jnp.concatenate([center[0:Q].reshape(rows, 2 * C), center[1 : Q + 1].reshape(rows, 2 * C)], axis=-1)
        for j in which:
            ACC[i, :, j * 2 * C : (j + 1) * 2 * C] += lax.dot_general(
                left, get_all(trio[j]), (((0,), (0,)), ((), ())), preferred_element_type=f32
            )

    def planes():
        for q in range(Q):
            for e in range(2):
                yield q, e, (q, slice(None), slice(e * C, e * C + C))

    def part(r, q, e):
        return r[q * W : (q + 1) * W, e * C : (e + 1) * C]

    def add8(total, v):
        return total + jnp.sum(v.reshape(-1, 8, C), axis=0)

    zero8 = jnp.zeros((8, C), f32)

    def act_of(h):
        return h + h * jnp.tanh(h)

    mean1 = mean[...]
    inv1 = 1.0 / std[...]

    def standard(m, at):
        return (XIN[(m, *at)].astype(f32) - mean1) * inv1

    def after_conv(b, v, m, r, cots):
        bias = vec(b, 3 * v) * 0.5
        t0, t1, t2, t3 = zero8, zero8, zero8, zero8
        for q, e, at in planes():
            h = part(r, q, e) + bias
            HS[(b * 2 + v, m, *at)] = h
            act = act_of(h)
            t0, t1 = add8(t0, act), add8(t1, act * act)
            if cots:
                dy = COT[(m, *at)].astype(f32)
                t2, t3 = add8(t2, dy), add8(t3, dy * act)
        sums = (fold_rows(t0), fold_rows(t1))
        if cots:
            sums += (fold_rows(t2), fold_rows(t3))
        return sums

    def send_block(views, b, t):
        @pl.when(sec == b)
        def _():
            for src, dst in views:
                pltpu.make_async_copy(src, dst, olsem.at[t]).start()

        @pl.when(sec != b)
        def _():
            for src, dst in views:
                to_sibling(src, dst, ossem.at[t], orsem.at[t])

    def sent_blocks(out, b, t):
        many = out.at[pl.ds(0, half)]

        @pl.when(sec == b)
        def _():
            wait(many, olsem.at[t])

        @pl.when(sec != b)
        def _():
            wait(many, ossem.at[t])

    def came_blocks(out, b, t):
        @pl.when(sec == b)
        def _():
            wait(out.at[pl.ds(0, half)], orsem.at[t])

    def xc(b, v, m):
        return XC.at[(b * 2 + v) * half + m]

    def trio_of(center):
        return LOW0.at[0], center, LOW0.at[2]

    low0 = tuple(LOW0.at[j] for j in range(3))
    low1 = tuple(LOW1.at[j] for j in range(3))

    def slot(stage, m):
        return (stage % 2) * half + m

    def stage0(m, carry):
        wait(XIN.at[m], isem.at[m])
        trio = trio_of(xc(0, 0, m))
        for q, e, at in planes():
            put(trio, q, e, standard(m, at))
        send_sums(slot(0, m), *after_conv(0, 0, m, conv(trio, WF.at[0]), False))
        return carry

    def stage_norm1(b, stage, m):
        sc, sh = norm_forward(b, 0, m, take_sums(slot(stage - 1, m)))
        if b == 1:
            wait(COT.at[m], isem.at[half + m])
        trio = trio_of(xc(b, 1, m))
        for q, e, at in planes():
            put(trio, q, e, act_of(HS[(b * 2, m, *at)]) * sc + sh)
        send_sums(slot(stage, m), *after_conv(b, 1, m, conv(trio, WF.at[b * 2 + 1]), b == 1))

    def stage1(m, carry):
        stage_norm1(0, 1, m)
        return carry

    def stage2(m, carry):
        sc, sh = norm_forward(0, 1, m, take_sums(slot(1, m)))
        center = xc(1, 0, m)
        trio = trio_of(center)
        for q, e, at in planes():
            put(trio, q, e, standard(m, at) + (act_of(HS[(1, m, *at)]) * sc + sh))
        send_sums(slot(2, m), *after_conv(1, 0, m, conv(trio, WF.at[2]), False))
        send_block(
            [
                (center.at[pl.ds(e, Q), :, pl.ds((1 - e) * C, C)], bo.at[sec * half + m, :, :, pl.ds(e * C, C)])
                for e in range(2)
            ],
            0,
            0,
        )
        return carry

    def stage3(m, carry):
        stage_norm1(1, 3, m)
        return carry

    def back_plane(trio, i, m, q, e, at, dy, coef):
        ca, cb, cc = coef
        h = HS[(i, m, *at)]
        u = 1.0 + jnp.tanh(h)
        act = h * u
        dp = (ca * dy + (cc * act + cb)) * (act + (0.5 * u) * (1.0 - act))
        put(trio, q, e, dp)
        return act, dp

    def step_e(b, stage, m, trio, before):
        total = take_sums(slot(stage - 1, m))
        if b == 1:
            sc, sh = norm_forward(1, 1, m, total)
            coef = norm_backward(1, 1, m, total[2:3], total[3:4])
        else:
            coef = norm_backward(0, 1, m, total[0:1], total[1:2])
            VACC[1, 0:1] += total[2:3]
        t0, t1, t2 = zero8, zero8, zero8
        i = b * 2 + 1
        wgrad(*before)
        for q, e, at in planes():
            act, dp = back_plane(trio, i, m, q, e, at, COT[(m, *at)].astype(f32), coef)
            t2 = add8(t2, dp)
            if b == 1:
                final = xc(1, 0, m)[spot(q, e)].astype(f32) + (act * sc + sh)
                XIN[(m, *at)] = final.astype(bf16)
        r = conv(trio, WD.at[i])
        for q, e, at in planes():
            dn = part(r, q, e)
            HS[(i, m, *at)] = dn
            t0, t1 = add8(t0, dn), add8(t1, dn * act_of(HS[(b * 2, m, *at)]))
        send_sums(slot(stage, m), fold_rows(t0), fold_rows(t1), fold_rows(t2))
        if b == 1:
            send_block([(XIN.at[m], bo.at[sec * half + m])], 1, 1)

    def coef_f(b, stage, m):
        total = take_sums(slot(stage - 1, m))
        VACC[b, 3:4] += total[2:3]
        return norm_backward(b, 0, m, total[0:1], total[1:2])

    def low_f(trio, b, m, coef):
        t2 = zero8
        for q, e, at in planes():
            t2 = add8(t2, back_plane(trio, b * 2, m, q, e, at, HS[(b * 2 + 1, m, *at)], coef)[1])
        return t2

    def step_f(b, stage, m, trio, before):
        coef = coef_f(1, stage, m)
        wgrad(*before)
        t2 = low_f(trio, 1, m, coef)
        r = conv(trio, WD.at[2])
        t0, t1 = zero8, zero8
        for q, e, at in planes():
            da = (COT[(m, *at)].astype(f32) + part(r, q, e)).astype(bf16)
            COT[(m, *at)] = da
            da = da.astype(f32)
            t0, t1 = add8(t0, da), add8(t1, da * act_of(HS[(1, m, *at)]))
        send_sums(slot(stage, m), fold_rows(t0), fold_rows(t1), fold_rows(t2))
        send_block([(COT.at[m], eg.at[sec * half + m])], 1, 2)

    def back_stage(step, b, stage, own, last, after):
        def pair(k, carry):
            m = 2 * k
            first = lax.div(1, k + 1)
            i = own + (last - own) * first
            x = own * half + m - 1 + ((last - own) * half + half) * first
            step(b, stage, m, low0, (i, XC.at[x], low1))
            step(b, stage, m + 1, low1, (own, xc(own // 2, own % 2, m), low0))
            for at, body in after:
                pl.when(k == at)(body)
            return carry

        lax.fori_loop(0, half // 2, pair, 0)

    def buffers(x):
        if x == 0:
            return PS2, GS2, GR2, GP2, GO2
        return PS1.at[x - 1], GS1.at[x - 1], GR1.at[x - 1], GP1.at[x - 1], GO1.at[x - 1]

    def taps(b, x):
        a = ACC.at[b * 2 + (1 if x == 0 else 0)]
        for i in range(3):
            for j in range(3) if x == 0 else (x - 1,):
                out = None
                for t in range(2):
                    for s in range(2):
                        e = 2 * t + s - i
                        if 0 <= e <= 1:
                            r = (2 * t + s) * C
                            c = ((2 - j) * 2 + e) * C
                            d = a[r : r + C, c : c + C]
                            out = d if out is None else out + d
                yield (i * 3 + j if x == 0 else i) * C, out

    def to_pair(b, x):
        ps, _, gr, _, _ = buffers(x)

        @pl.when(sec != b)
        def _():
            for row, val in taps(b, x):
                ps[row : row + C] = val.astype(bf16)
            to_sibling(ps, gr, gsend.at[x, 0], grecv.at[x, 0])

    def piece_size(x):
        return GP2.shape[1] if x == 0 else GP1.shape[2]

    def owners(x):
        k = (GO2.shape[0] if x == 0 else GO1.shape[1]) // piece_size(x)
        return k, (n - k) // 2

    def piece(ref, x, p):
        size = piece_size(x)
        return ref.at[pl.ds(pl.multiple_of(p * size, 16), size)]

    def span(ref, x, k):
        return ref.at[pl.ds(0, k * piece_size(x))]

    def to_owners(b, x):
        _, gs, gr, gp, _ = buffers(x)
        k, first = owners(x)

        @pl.when(sec == b)
        def _():
            wait(gr, grecv.at[x, 0])
            for row, val in taps(b, x):
                gs[row : row + C] = (val + gr[row : row + C].astype(f32)).astype(bf16)
            for d in range(k):
                p = lax.rem(me + d, k)

                @pl.when(first + p == me)
                def _():
                    gp[me] = piece(gs, x, p)[...]

                @pl.when(first + p != me)
                def _():
                    pltpu.make_async_remote_copy(
                        piece(gs, x, p), gp.at[me], gsend.at[x, 1], grecv.at[x, 1],
                        device_id={"dp": first + p}, device_id_type=MESH,
                    ).start()

    def when_owner(b, x, mine, other):
        k, first = owners(x)
        own = (me >= first) & (me < first + k)
        pl.when((sec == b) & own)(mine)
        pl.when((sec == b) & jnp.logical_not(own))(other)

    def to_all(b, x):
        _, gs, _, gp, go = buffers(x)
        k, first = owners(x)

        def mine():
            if n > 1:
                wait(gp.at[pl.ds(0, n - 1)], grecv.at[x, 1])
            if k > 1:
                wait(span(gs, x, k - 1), gsend.at[x, 1])
            total = gp[0].astype(f32)
            for d in range(1, n):
                total = total + gp[d].astype(f32)
            at = piece(go, x, me - first)
            at[...] = total.astype(bf16)
            every_peer(
                lambda d: pltpu.make_async_remote_copy(
                    at, at, gsend.at[x, 2], grecv.at[x, 2], device_id=peer(d), device_id_type=MESH
                ).start()
            )

        when_owner(b, x, mine, lambda: wait(span(gs, x, k), gsend.at[x, 1]))

    def finish(b, x):
        ps, _, _, gp, go = buffers(x)
        k, _ = owners(x)

        def mine():
            if k > 1:
                wait(span(go, x, k - 1), grecv.at[x, 2])
            if n > 1:
                wait(gp.at[pl.ds(0, n - 1)], gsend.at[x, 2])

        when_owner(b, x, mine, lambda: wait(span(go, x, k), grecv.at[x, 2]))

        @pl.when(sec != b)
        def _():
            wait(ps, gsend.at[x, 0])

    @pl.when(sec != 0)
    def _():
        wait(WR.at[0, 0], wrsem.at[0])

    prep_forward(0, 0)
    wait(PV.at[0], wrsem.at[2])
    lax.fori_loop(0, half, stage0, 0)

    @pl.when(sec == 0)
    def _():
        wait(WR.at[0, 0], wrsem.at[0])

    wait(WR.at[0, 1], wrsem.at[1])
    for v in range(2):
        wait(WR.at[0, 0], wssem.at[v])
    wait(PV.at[0], wssem.at[2])
    prep_forward(0, 1)
    prep_backward(0, 0)
    lax.fori_loop(0, half, stage1, 0)
    prep_forward(1, 0)
    prep_backward(0, 1)
    lax.fori_loop(0, half, stage2, 0)
    prep_forward(1, 1)
    prep_backward(1, 1)
    lax.fori_loop(0, half, stage3, 0)
    prep_backward(1, 0)
    w1_parts = (1, 2, 3)
    back_stage(step_e, 1, 4, 3, 3, [])
    back_stage(
        step_f, 1, 5, 2, 3, [(0, lambda: to_pair(1, 0)), (half // 2 - 1, lambda: to_owners(1, 0))]
    )
    back_stage(
        step_e,
        0,
        6,
        1,
        2,
        [
            (0, lambda: [to_pair(1, x) for x in w1_parts] and None),
            (half // 2 - 1, lambda: [to_owners(1, x) for x in w1_parts] and to_all(1, 0)),
        ],
    )
    sent_blocks(bo, 0, 0)

    def last_trio(m):
        return xc(1, 1, m), xc(0, 1, m), xc(1, 0, m)

    for m in range(half):
        coef = coef_f(0, 7, m)
        if m == 0:
            wgrad(1, xc(0, 1, half - 1), low1)
        else:
            wgrad(0, xc(0, 0, m - 1), last_trio(m - 1), (2, 1))
        send_sums(slot(7, m), fold_rows(low_f(last_trio(m), 0, m, coef)))
        if m == 0:
            to_pair(0, 0)
        if m == 2:
            to_owners(0, 0)
    wgrad(0, xc(0, 0, half - 1), last_trio(half - 1), (2, 1))
    to_pair(0, 1)
    to_pair(0, 2)

    def last_column(m, carry):
        wgrad(0, xc(0, 0, m), last_trio(m), (0,))
        return carry

    lax.fori_loop(0, half, last_column, 0)
    to_pair(0, 3)
    to_owners(0, 1)
    to_owners(0, 2)
    for x in w1_parts:
        to_all(1, x)
    sent_blocks(eg, 1, 2)

    def stage8(m, carry):
        r = conv(last_trio(m), WD.at[0])
        for q, e, at in planes():
            da = (COT[(m, *at)].astype(f32) + part(r, q, e)) * inv1
            COT[(m, *at)] = da.astype(bf16)
        send_block([(COT.at[m], eg.at[sec * half + m])], 0, 3)

        @pl.when(m == 0)
        def _():
            to_owners(0, 3)

        @pl.when(m == 2)
        def _():
            to_all(0, 0)

        return carry

    lax.fori_loop(0, half, stage8, 0)

    for m in range(half):
        VACC[0, 0:1] += take_sums(slot(7, m))[0:1]
    to_sibling(VACC.at[sib], VR, vsem.at[0], vsem.at[1])
    for x in w1_parts:
        to_all(0, x)
    wait(VR, vsem.at[1])
    wait(VR, vsem.at[0])
    gvec[...] = VACC[sec] + VR[...]
    sent_blocks(bo, 1, 1)
    sent_blocks(eg, 0, 3)
    came_blocks(bo, 0, 0)
    came_blocks(bo, 1, 1)
    came_blocks(eg, 1, 2)
    came_blocks(eg, 0, 3)
    for b in (1, 0):
        for x in range(4):
            finish(b, x)


def writer(*refs):
    bo_in, eg_in, go2, go1, gvec, bo, eg, gw1, gw2 = refs[:9]
    vecs, sem = refs[9:15], refs[15]
    copies = []
    for k, (src, dst) in enumerate(((bo_in, bo), (eg_in, eg))):
        for m in range(src.shape[0]):
            for e in range(2):
                copies.append(
                    pltpu.make_async_copy(src.at[m, :, :, pl.ds(e * C, C)], dst.at[m, :, e], sem.at[k, m, e])
                )
                copies[-1].start()
    for k in range(9):
        gw2[k] = go2[k * C : (k + 1) * C].astype(f32)
        gw1[k] = go1[k % 3, k // 3 * C : (k // 3 + 1) * C].astype(f32)
    for k, ref in enumerate(vecs):
        ref[...] = gvec[k : k + 1]
    for copy in copies:
        copy.wait()


def solution(mesh):
    n = mesh.shape["dp"]
    size2, own2 = piece_rows(9 * C, n)
    size1, own1 = piece_rows(3 * C, n)

    def per_device(inputs, channel_mean, channel_std, cotangent, conv_w1, conv_b1, bn_gain1, bn_shift1, conv_w2, conv_b2, bn_gain2, bn_shift2):
        micro, _, H, W, _ = inputs.shape
        half = micro // 2
        Q = H // 2
        field = (micro, Q, 2, W, C)
        pairs = (micro, Q, W, 2 * C)
        anywhere = pl.BlockSpec(memory_space=pl.ANY)
        vmem = pl.BlockSpec(memory_space=pltpu.VMEM)
        D = pltpu.SemaphoreType.DMA
        V = pltpu.VMEM
        mid = pl.pallas_call(
            functools.partial(kernel, n),
            out_shape=[
                V(pairs, bf16),
                V(pairs, bf16),
                V((own2 * size2, C), bf16),
                V((3, own1 * size1, C), bf16),
                V((8, C), f32),
            ],
            in_specs=[anywhere, anywhere, vmem, vmem, anywhere, vmem, vmem, vmem, anywhere, vmem, vmem, vmem],
            out_specs=[vmem] * 5,
            scratch_shapes=[
                V((half, Q, W, 2 * C), bf16),
                V((half, Q, W, 2 * C), bf16),
                V((4 * half, Q + 1, W, 2 * C), bf16),
                V((3, Q + 1, W, 2 * C), bf16),
                V((3, Q + 1, W, 2 * C), bf16),
                V((4, half, Q, W, 2 * C), f32),
                V((4, 3, 2, 2 * C, 2 * C), bf16),
                V((4, 3, 2, 2 * C, 2 * C), bf16),
                V((4, 4 * C, 6 * C), f32),
                V((2, 2, 9, C, C), bf16),
                V((2, 8, C), f32),
                V((4, half, 8, C), f32),
                V((2, 8, C), f32),
                V((8, C), f32),
                V((2 * half, 4, C), f32),
                V((2 * half, n, 4, C), f32),
                V((own2 * size2, C), bf16),
                V((3, own1 * size1, C), bf16),
                V((own2 * size2, C), bf16),
                V((3, own1 * size1, C), bf16),
                V((own2 * size2, C), bf16),
                V((3, own1 * size1, C), bf16),
                V((n, size2, C), bf16),
                V((3, n, size1, C), bf16),
                D((2 * half,)),
                D((2,)),
                D((3,)),
                D((3,)),
                D((2 * half,)),
                D((2 * half,)),
                D((4,)),
                D((4,)),
                D((4,)),
                D((4, 3)),
                D((4, 3)),
                D((2,)),
            ],
            compiler_params=pltpu.CompilerParams(
                collective_id=0, has_side_effects=True, vmem_limit_bytes=VMEM_LIMIT
            ),
        )(
            inputs.reshape(field),
            cotangent.reshape(field),
            channel_mean[None],
            channel_std[None],
            conv_w1.reshape(9, C, C),
            conv_b1,
            bn_gain1,
            bn_shift1,
            conv_w2.reshape(9, C, C),
            conv_b2,
            bn_gain2,
            bn_shift2,
        )
        bo, eg, gw1, gw2, *vecs = pl.pallas_call(
            writer,
            out_shape=[
                jax.ShapeDtypeStruct(field, bf16),
                jax.ShapeDtypeStruct(field, bf16),
                jax.ShapeDtypeStruct((9, C, C), f32),
                jax.ShapeDtypeStruct((9, C, C), f32),
            ]
            + [jax.ShapeDtypeStruct((1, C), f32)] * 6,
            in_specs=[vmem] * 5,
            out_specs=[anywhere, anywhere] + [vmem] * 8,
            scratch_shapes=[D((2, micro, 2))],
            compiler_params=pltpu.CompilerParams(vmem_limit_bytes=8 * 2**20),
        )(*[pltpu.with_memory_space_constraint(v, pltpu.VMEM) for v in mid])
        whole = (1, micro, 1, H, W, C)
        kernel_shape = (1, 3, 3, C, C)
        return (
            bo.reshape(whole),
            eg.reshape(whole),
            gw1.reshape(kernel_shape),
            vecs[0],
            vecs[1],
            vecs[2],
            gw2.reshape(kernel_shape),
            vecs[3],
            vecs[4],
            vecs[5],
        )

    in_specs = (
        P(None, "dp", None, None, None),
        P(),
        P(),
        P(None, "dp", None, None, None),
        P("section", None, None, None, None),
        P("section", None),
        P("section", None),
        P("section", None),
        P("section", None, None, None, None),
        P("section", None),
        P("section", None),
        P("section", None),
    )
    out_specs = (
        P("section", None, "dp", None, None, None),
        P("section", None, "dp", None, None, None),
        P("section", None, None, None, None),
        P("section", None),
        P("section", None),
        P("section", None),
        P("section", None, None, None, None),
        P("section", None),
        P("section", None),
        P("section", None),
    )
    return jax.shard_map(per_device, mesh=mesh, in_specs=in_specs, out_specs=out_specs, check_vma=False)
```

```python
import functools

import jax
import jax.numpy as jnp
from jax import lax
from jax.experimental import pallas as pl
from jax.experimental.pallas import tpu as pltpu
from jax.sharding import PartitionSpec as P

norm_eps = 1e-05
MESH = pl.DeviceIdType.MESH
bf16 = jnp.bfloat16
f32 = jnp.float32
C = 128
VMEM_LIMIT = 55 * 2**20


def dot(a, b):
    return jnp.dot(a, b, preferred_element_type=f32)


def fold_rows(v):
    return jnp.sum(v, axis=0, keepdims=True)


PARTS = ((1, (0, 1, 2)), (0, (0, 1)), (0, (2,)))


def part_rows(x):
    return 3 * len(PARTS[x][1]) * C


def plane_of(n):
    plane = min(d for d in range(1, n + 1) if n % d == 0 and d * d >= n)
    planes = n // plane
    return plane, planes, min(2, max(1, planes // 2))


def piece_rows(rows, n):
    plane, _, owning = plane_of(n)
    owners = plane * owning
    return -(-rows // owners // 16) * 16, owners


def kernel(n, *refs):
    (
        inp, cot, mean, std, w1, b1, g1, s1, w2, b2, g2, s2,
        bo, eg, GO0, GO1, GO2, gvec,
        XIN, COT, XC, LOW0, LOW1, HS, WF, WD, ACC, PV, ST, VACC, VR,
        MSG, SLOT, PS0, PS1, PS2, GS0, GS1, GS2, GR0, GR1, GR2, GP0, GP1, GP2,
        isem, wlsem, wssem, wrsem, msend, mrecv, olsem, ossem, orsem, gsend, grecv, vsem,
    ) = refs
    micro = inp.shape[0]
    half = micro // 2
    Q = inp.shape[1]
    W = inp.shape[3]
    rows = Q * W
    count = float(2 * rows * n)

    plane, all_planes, owning = plane_of(n)
    first_plane = (all_planes - owning) // 2

    me = lax.axis_index("dp")
    my_plane, my_line = me // plane, me % plane
    my_piece = my_line * owning + my_plane - first_plane
    is_owner = (my_plane >= first_plane) & (my_plane < first_plane + owning)
    sec = lax.axis_index("section")
    sib = 1 - sec

    def peer(d):
        return {"dp": lax.rem(me + d, n)}

    def every_peer(body):
        if n <= 16:
            for d in range(1, n):
                body(d)
        else:
            lax.fori_loop(1, n, lambda d, carry: (body(d), carry)[1], 0)

    def wait(ref, sem):
        pltpu.make_async_copy(ref, ref, sem).wait()

    def to_sibling(src, dst, send, recv):
        pltpu.make_async_remote_copy(
            src, dst, send, recv, device_id={"section": sib}, device_id_type=MESH
        ).start()

    barrier = pltpu.get_barrier_semaphore()
    pl.semaphore_signal(barrier, inc=1, device_id={"section": sib}, device_id_type=MESH)
    every_peer(lambda d: pl.semaphore_signal(barrier, inc=1, device_id=peer(d), device_id_type=MESH))

    def raw(b, v):
        return XC.at[3 * half + 2 * b + v, pl.ds(0, 9)]

    def raw_tap(b, v, k):
        tap = raw(b, v)[k]
        return jnp.concatenate([tap[:, :C], tap[:, C:]], axis=0)

    for v, ref in enumerate((w1, w2)):
        for e in range(2):
            pltpu.make_async_copy(ref.at[:, e], raw(sec, v).at[:, :, pl.ds(e * C, C)], wlsem.at[v]).start()
    for src, dst, at in ((inp, XIN, 0), (cot, COT, half)):
        for m in range(half):
            for e in range(2):
                pltpu.make_async_copy(
                    src.at[sec * half + m, :, e], dst.at[m, :, :, pl.ds(e * C, C)], isem.at[at + m]
                ).start()

    for v, ref in enumerate((b1, g1, s1, b2, g2, s2)):
        PV[sec, v : v + 1] = ref[...]

    halo = jnp.zeros((W, C), bf16)
    for j in range(3):
        LOW0[j, 0, :, 0:C] = halo
        LOW0[j, Q, :, C : 2 * C] = halo
    LOW1[...] = jnp.zeros(LOW1.shape, bf16)

    def zero_halo(i, carry):
        XC[i, 0, :, 0:C] = halo
        XC[i, Q, :, C : 2 * C] = halo
        return carry

    lax.fori_loop(0, 3 * half, zero_halo, 0)
    empty = jnp.zeros((C, C), bf16)
    for i in range(4):
        ACC[i] = jnp.zeros(ACC.shape[1:], f32)
        for j in range(3):
            for ref in (WF, WD):
                ref[i, j, 0, 0:C, C : 2 * C] = empty
                ref[i, j, 1, C : 2 * C, 0:C] = empty
    VACC[...] = jnp.zeros(VACC.shape, f32)
    for ref in (PS0, PS1, PS2, GS0, GS1, GS2):
        ref[...] = jnp.zeros(ref.shape, bf16)

    pl.semaphore_wait(barrier, n)

    to_sibling(PV.at[sec], PV.at[sec], wssem.at[2], wrsem.at[2])
    for v in range(2):
        wait(raw(sec, v), wlsem.at[v])
        to_sibling(raw(sec, v), raw(sec, v), wssem.at[v], wrsem.at[v])

    def blocks():
        for j in range(3):
            for t in range(2):
                for s in range(2):
                    for e in range(2):
                        i = 2 * t + s - e
                        if 0 <= i <= 2:
                            yield i, j, t, slice(s * C, s * C + C), slice(e * C, e * C + C)

    def prep_forward(b, v):
        for i, j, t, r, c in blocks():
            WF[b * 2 + v, j, t, r, c] = (raw_tap(b, v, i * 3 + j).astype(f32) * 0.5).astype(bf16)

    def prep_backward(b, v):
        for i, j, t, r, c in blocks():
            WD[b * 2 + v, j, t, r, c] = raw_tap(b, v, (2 - i) * 3 + 2 - j).T

    def vec(b, v):
        return PV[b, v : v + 1]

    def send_sums(i, *sums):
        for r, v in enumerate(sums):
            MSG[i, r : r + 1] = v
        SLOT[i, me] = MSG[i]
        every_peer(
            lambda d: pltpu.make_async_remote_copy(
                MSG.at[i], SLOT.at[i, me], msend.at[i], mrecv.at[i], device_id=peer(d), device_id_type=MESH
            ).start()
        )

    def sum_slots(i):
        total = SLOT[i, 0]
        for d in range(1, n):
            total = total + SLOT[i, d]
        return total

    def take_sums(i):
        if n > 1:
            many = SLOT.at[i, pl.ds(0, n - 1)]
            wait(many, mrecv.at[i])
            wait(many, msend.at[i])
        return sum_slots(i)

    def norm_forward(b, v, m, total):
        mu = total[0:1] / count
        rstd = lax.rsqrt(total[1:2] / count - mu * mu + norm_eps)
        ST[b * 2 + v, m, 0:1] = mu
        ST[b * 2 + v, m, 1:2] = rstd
        sc = vec(b, 1 + 3 * v) * rstd
        return sc, vec(b, 2 + 3 * v) - mu * sc

    def norm_backward(b, v, m, shift_sum, prod_sum):
        mu = ST[b * 2 + v, m, 0:1]
        rstd = ST[b * 2 + v, m, 1:2]
        gain_sum = rstd * (prod_sum - mu * shift_sum)
        VACC[b, 3 * v + 1 : 3 * v + 2] += gain_sum
        VACC[b, 3 * v + 2 : 3 * v + 3] += shift_sum
        ca = vec(b, 1 + 3 * v) * rstd
        cc = -ca * rstd * gain_sum / count
        cb = -ca * shift_sum / count - cc * mu
        return ca, cb, cc

    def spot(q, e):
        return q + e, slice(None), slice((1 - e) * C, (2 - e) * C)

    def put(trio, q, e, v):
        for j, ref in enumerate(trio):
            ref[spot(q, e)] = (v if j == 1 else pltpu.roll(v, 1 if j == 0 else W - 1, 0)).astype(bf16)

    def get_all(center):
        both = [center[0:Q, :, C : 2 * C], center[1 : Q + 1, :, 0:C]]
        return jnp.concatenate(both, axis=-1).reshape(rows, 2 * C)

    def conv(trio, w):
        acc = None
        for j, ref in enumerate(trio):
            for t in range(2):
                d = dot(ref[t : t + Q].reshape(rows, 2 * C), w[j, t])
                acc = d if acc is None else acc + d
        return acc

    def wgrad(i, center, trio, which=(0, 1, 2)):
        left = jnp.concatenate([center[0:Q].reshape(rows, 2 * C), center[1 : Q + 1].reshape(rows, 2 * C)], axis=-1)
        for j in which:
            ACC[i, :, j * 2 * C : (j + 1) * 2 * C] += lax.dot_general(
                left, get_all(trio[j]), (((0,), (0,)), ((), ())), preferred_element_type=f32
            )

    def planes():
        for q in range(Q):
            for e in range(2):
                yield q, e, (q, slice(None), slice(e * C, e * C + C))

    def part(r, q, e):
        return r[q * W : (q + 1) * W, e * C : (e + 1) * C]

    def add8(total, v):
        return total + jnp.sum(v.reshape(-1, 8, C), axis=0)

    zero8 = jnp.zeros((8, C), f32)

    def act_of(h):
        return h + h * jnp.tanh(h)

    mean1 = mean[...]
    inv1 = 1.0 / std[...]

    def standard(m, at):
        return (XIN[(m, *at)].astype(f32) - mean1) * inv1

    def after_conv(b, v, m, r, cots):
        bias = vec(b, 3 * v) * 0.5
        t0, t1, t2, t3 = zero8, zero8, zero8, zero8
        for q, e, at in planes():
            h = part(r, q, e) + bias
            HS[(b * 2 + v, m, *at)] = h
            act = act_of(h)
            t0, t1 = add8(t0, act), add8(t1, act * act)
            if cots:
                dy = COT[(m, *at)].astype(f32)
                t2, t3 = add8(t2, dy), add8(t3, dy * act)
        sums = (fold_rows(t0), fold_rows(t1))
        if cots:
            sums += (fold_rows(t2), fold_rows(t3))
        return sums

    def send_block(views, b, t):
        @pl.when(sec == b)
        def _():
            for src, dst in views:
                pltpu.make_async_copy(src, dst, olsem.at[t]).start()

        @pl.when(sec != b)
        def _():
            for src, dst in views:
                to_sibling(src, dst, ossem.at[t], orsem.at[t])

    def sent_blocks(out, b, t):
        many = out.at[pl.ds(0, half)]

        @pl.when(sec == b)
        def _():
            wait(many, olsem.at[t])

        @pl.when(sec != b)
        def _():
            wait(many, ossem.at[t])

    def came_blocks(out, b, t):
        @pl.when(sec == b)
        def _():
            wait(out.at[pl.ds(0, half)], orsem.at[t])

    def xc(b, v, m):
        return XC.at[(b * 2 + v) * half + m]

    def trio_of(center):
        return LOW0.at[0], center, LOW0.at[2]

    low0 = tuple(LOW0.at[j] for j in range(3))
    low1 = tuple(LOW1.at[j] for j in range(3))

    def slot(stage, m):
        return (stage % 2) * half + m

    def stage0(m, carry):
        wait(XIN.at[m], isem.at[m])
        trio = trio_of(xc(0, 0, m))
        for q, e, at in planes():
            put(trio, q, e, standard(m, at))
        send_sums(slot(0, m), *after_conv(0, 0, m, conv(trio, WF.at[0]), False))
        return carry

    def stage_norm1(b, stage, m):
        sc, sh = norm_forward(b, 0, m, take_sums(slot(stage - 1, m)))
        if b == 1:
            wait(COT.at[m], isem.at[half + m])
        trio = trio_of(xc(b, 1, m))
        for q, e, at in planes():
            put(trio, q, e, act_of(HS[(b * 2, m, *at)]) * sc + sh)
        send_sums(slot(stage, m), *after_conv(b, 1, m, conv(trio, WF.at[b * 2 + 1]), b == 1))

    def stage1(m, carry):
        stage_norm1(0, 1, m)
        return carry

    def stage2(m, carry):
        sc, sh = norm_forward(0, 1, m, take_sums(slot(1, m)))
        center = xc(1, 0, m)
        trio = trio_of(center)
        for q, e, at in planes():
            put(trio, q, e, standard(m, at) + (act_of(HS[(1, m, *at)]) * sc + sh))
        send_sums(slot(2, m), *after_conv(1, 0, m, conv(trio, WF.at[2]), False))
        send_block(
            [
                (center.at[pl.ds(e, Q), :, pl.ds((1 - e) * C, C)], bo.at[sec * half + m, :, :, pl.ds(e * C, C)])
                for e in range(2)
            ],
            0,
            0,
        )
        return carry

    def stage3(m, carry):
        stage_norm1(1, 3, m)
        return carry

    def back_plane(trio, i, m, q, e, at, dy, coef):
        ca, cb, cc = coef
        h = HS[(i, m, *at)]
        u = 1.0 + jnp.tanh(h)
        act = h * u
        dp = (ca * dy + (cc * act + cb)) * (act + (0.5 * u) * (1.0 - act))
        put(trio, q, e, dp)
        return act, dp

    def step_e(b, stage, m, trio, before):
        total = take_sums(slot(stage - 1, m))
        if b == 1:
            sc, sh = norm_forward(1, 1, m, total)
            coef = norm_backward(1, 1, m, total[2:3], total[3:4])
        else:
            coef = norm_backward(0, 1, m, total[0:1], total[1:2])
            VACC[1, 0:1] += total[2:3]
        t0, t1, t2 = zero8, zero8, zero8
        i = b * 2 + 1
        wgrad(*before)
        for q, e, at in planes():
            act, dp = back_plane(trio, i, m, q, e, at, COT[(m, *at)].astype(f32), coef)
            t2 = add8(t2, dp)
            if b == 1:
                final = xc(1, 0, m)[spot(q, e)].astype(f32) + (act * sc + sh)
                XIN[(m, *at)] = final.astype(bf16)
        r = conv(trio, WD.at[i])
        for q, e, at in planes():
            dn = part(r, q, e)
            HS[(i, m, *at)] = dn
            t0, t1 = add8(t0, dn), add8(t1, dn * act_of(HS[(b * 2, m, *at)]))
        send_sums(slot(stage, m), fold_rows(t0), fold_rows(t1), fold_rows(t2))
        if b == 1:
            send_block([(XIN.at[m], bo.at[sec * half + m])], 1, 1)

    def coef_f(b, stage, m):
        total = take_sums(slot(stage - 1, m))
        VACC[b, 3:4] += total[2:3]
        return norm_backward(b, 0, m, total[0:1], total[1:2])

    def low_f(trio, b, m, coef):
        t2 = zero8
        for q, e, at in planes():
            t2 = add8(t2, back_plane(trio, b * 2, m, q, e, at, HS[(b * 2 + 1, m, *at)], coef)[1])
        return t2

    def step_f(b, stage, m, trio, before):
        coef = coef_f(1, stage, m)
        wgrad(*before)
        t2 = low_f(trio, 1, m, coef)
        r = conv(trio, WD.at[2])
        t0, t1 = zero8, zero8
        for q, e, at in planes():
            da = (COT[(m, *at)].astype(f32) + part(r, q, e)).astype(bf16)
            COT[(m, *at)] = da
            da = da.astype(f32)
            t0, t1 = add8(t0, da), add8(t1, da * act_of(HS[(1, m, *at)]))
        send_sums(slot(stage, m), fold_rows(t0), fold_rows(t1), fold_rows(t2))
        send_block([(COT.at[m], eg.at[sec * half + m])], 1, 2)

    def back_stage(step, b, stage, own, last, after):
        def hooks(k, odd):
            for m, body in after:
                if m % 2 == odd:
                    pl.when(k == m // 2)(body)

        def pair(k, carry):
            m = 2 * k
            first = lax.div(1, k + 1)
            i = own + (last - own) * first
            x = own * half + m - 1 + ((last - own) * half + half) * first
            step(b, stage, m, low0, (i, XC.at[x], low1))
            hooks(k, 0)
            step(b, stage, m + 1, low1, (own, xc(own // 2, own % 2, m), low0))
            hooks(k, 1)
            return carry

        lax.fori_loop(0, half // 2, pair, 0)

    def buffers(x):
        return ((PS0, PS1, PS2)[x], (GS0, GS1, GS2)[x], (GR0, GR1, GR2)[x], (GP0, GP1, GP2)[x], (GO0, GO1, GO2)[x])

    def taps(b, x):
        v, columns = PARTS[x]
        a = ACC.at[b * 2 + v]
        for i in range(3):
            for at, j in enumerate(columns):
                out = None
                for t in range(2):
                    for s in range(2):
                        e = 2 * t + s - i
                        if 0 <= e <= 1:
                            r = (2 * t + s) * C
                            c = ((2 - j) * 2 + e) * C
                            d = a[r : r + C, c : c + C]
                            out = d if out is None else out + d
                yield (i * len(columns) + at) * C, out

    def to_pair(b, x):
        ps, _, gr, _, _ = buffers(x)

        @pl.when(sec != b)
        def _():
            for row, val in taps(b, x):
                ps[row : row + C] = val.astype(bf16)
            to_sibling(ps, gr, gsend.at[x, 0], grecv.at[x, 0])

    def piece_size(x):
        return buffers(x)[3].shape[1]

    owners = plane * owning

    def piece(ref, x, p):
        size = piece_size(x)
        return ref.at[pl.ds(pl.multiple_of(p * size, 16), size)]

    def span(ref, x, k):
        return ref.at[pl.ds(0, k * piece_size(x))]

    def when_owner(b, mine, other):
        pl.when((sec == b) & is_owner)(mine)
        pl.when((sec == b) & jnp.logical_not(is_owner))(other)

    def to_owners(b, x):
        _, gs, gr, gp, _ = buffers(x)

        @pl.when(sec == b)
        def _():
            wait(gr, grecv.at[x, 0])
            for row, val in taps(b, x):
                gs[row : row + C] = (val + gr[row : row + C].astype(f32)).astype(bf16)

        def send(p):
            to = (first_plane + p % owning) * plane + p // owning
            pltpu.make_async_remote_copy(
                piece(gs, x, p), gp.at[me], gsend.at[x, 1], grecv.at[x, 1], device_id={"dp": to}, device_id_type=MESH
            ).start()

        def mine():
            for d in range(1, owners):
                send(lax.rem(my_piece + d, owners))
            gp[me] = piece(gs, x, my_piece)[...]

        def other():
            for d in range(owners):
                send(lax.rem(me + d, owners))

        when_owner(b, mine, other)

    def to_all(b, x, direct):
        _, gs, _, gp, go = buffers(x)

        def mine():
            if n > 1:
                wait(gp.at[pl.ds(0, n - 1)], grecv.at[x, 1])
            if owners > 1:
                wait(span(gs, x, owners - 1), gsend.at[x, 1])
            total = gp[0].astype(f32)
            for d in range(1, n):
                total = total + gp[d].astype(f32)
            at = piece(go, x, my_piece)
            at[...] = total.astype(bf16)

            def send(to):
                pltpu.make_async_remote_copy(
                    at, at, gsend.at[x, 2], grecv.at[x, 2], device_id=to, device_id_type=MESH
                ).start()

            if direct:
                every_peer(lambda d: send(peer(d)))
            else:
                for d in range(1, all_planes):
                    send({"dp": lax.rem(my_plane + d, all_planes) * plane + my_line})

        when_owner(b, mine, lambda: wait(span(gs, x, owners), gsend.at[x, 1]))

    def got_pieces(b, x, k):
        go = buffers(x)[4]

        def mine():
            if k > 1:
                wait(span(go, x, k - 1), grecv.at[x, 2])

        when_owner(b, mine, lambda: wait(span(go, x, k), grecv.at[x, 2]))

    def spread(b, x):
        go = buffers(x)[4]
        got_pieces(b, x, owning)
        size = piece_size(x) * owning
        at = go.at[pl.ds(pl.multiple_of(my_line * size, 16), size)]

        @pl.when(sec == b)
        def _():
            for d in range(1, plane):
                pltpu.make_async_remote_copy(
                    at, at, gsend.at[x, 3], grecv.at[x, 3],
                    device_id={"dp": my_plane * plane + lax.rem(my_line + d, plane)}, device_id_type=MESH,
                ).start()

    def finish(b, x, direct):
        ps, _, _, gp, go = buffers(x)
        copies = n - 1 if direct else all_planes - 1
        if direct:
            got_pieces(b, x, owners)

        @pl.when(sec == b)
        def _():
            if not direct and plane > 1:
                many = span(go, x, owning * (plane - 1))
                wait(many, grecv.at[x, 3])
                wait(many, gsend.at[x, 3])

        if copies > 0:
            pl.when((sec == b) & is_owner)(lambda: wait(gp.at[pl.ds(0, copies)], gsend.at[x, 2]))

        @pl.when(sec != b)
        def _():
            wait(ps, gsend.at[x, 0])

    @pl.when(sec != 0)
    def _():
        wait(raw(0, 0), wrsem.at[0])

    prep_forward(0, 0)
    wait(PV.at[0], wrsem.at[2])
    lax.fori_loop(0, half, stage0, 0)

    @pl.when(sec == 0)
    def _():
        wait(raw(0, 0), wrsem.at[0])

    wait(raw(0, 1), wrsem.at[1])
    for v in range(2):
        wait(raw(0, 0), wssem.at[v])
    wait(PV.at[0], wssem.at[2])
    prep_forward(0, 1)
    prep_backward(0, 0)
    lax.fori_loop(0, half, stage1, 0)
    prep_forward(1, 0)
    prep_backward(0, 1)
    lax.fori_loop(0, half, stage2, 0)
    prep_forward(1, 1)
    prep_backward(1, 1)
    prep_backward(1, 0)
    lax.fori_loop(3 * half, 4 * half, zero_halo, 0)
    lax.fori_loop(0, half, stage3, 0)
    w1_parts = (1, 2)
    back_stage(step_e, 1, 4, 3, 3, [])
    back_stage(step_f, 1, 5, 2, 3, [(0, lambda: to_pair(1, 0)), (1, lambda: to_owners(1, 0))])

    def every_part(phase, b):
        for x in w1_parts:
            phase(b, x)

    back_stage(
        step_e,
        0,
        6,
        1,
        2,
        [
            (0, lambda: every_part(to_pair, 1)),
            (1, lambda: every_part(to_owners, 1)),
            (1, lambda: to_all(1, 0, False)),
        ],
    )
    sent_blocks(bo, 0, 0)

    def last_trio(m):
        return xc(1, 1, m), xc(0, 1, m), xc(1, 0, m)

    for m in range(half):
        coef = coef_f(0, 7, m)
        if m == 0:
            wgrad(1, xc(0, 1, half - 1), low1)
        else:
            wgrad(0, xc(0, 0, m - 1), last_trio(m - 1), (2, 1))
        send_sums(slot(7, m), fold_rows(low_f(last_trio(m), 0, m, coef)))
        if m == 0:
            to_pair(0, 0)
        if m == 1:
            to_owners(0, 0)
            spread(1, 0)
        if m == half - 1:
            for x in w1_parts:
                to_all(1, x, False)
    wgrad(0, xc(0, 0, half - 1), last_trio(half - 1), (2, 1))
    to_pair(0, 1)

    def last_column(m, carry):
        wgrad(0, xc(0, 0, m), last_trio(m), (0,))
        return carry

    lax.fori_loop(0, half, last_column, 0)
    to_pair(0, 2)
    to_owners(0, 1)
    sent_blocks(eg, 1, 2)

    def stage8(m, carry):
        r = conv(last_trio(m), WD.at[0])
        for q, e, at in planes():
            da = (COT[(m, *at)].astype(f32) + part(r, q, e)) * inv1
            COT[(m, *at)] = da.astype(bf16)
        send_block([(COT.at[m], eg.at[sec * half + m])], 0, 3)

        @pl.when(m == 0)
        def _():
            to_owners(0, 2)

        @pl.when(m == 1)
        def _():
            to_all(0, 0, False)
            every_part(spread, 1)

        return carry

    lax.fori_loop(0, half, stage8, 0)

    for m in range(half):
        VACC[0, 0:1] += take_sums(slot(7, m))[0:1]
    to_sibling(VACC.at[sib], VR, vsem.at[0], vsem.at[1])
    spread(0, 0)
    for x in w1_parts:
        to_all(0, x, True)
    wait(VR, vsem.at[1])
    wait(VR, vsem.at[0])
    gvec[...] = VACC[sec] + VR[...]
    sent_blocks(bo, 1, 1)
    sent_blocks(eg, 0, 3)
    came_blocks(bo, 0, 0)
    came_blocks(bo, 1, 1)
    came_blocks(eg, 1, 2)
    came_blocks(eg, 0, 3)
    for b in (1, 0):
        for x in range(3):
            finish(b, x, b == 0 and x > 0)


def writer(*refs):
    bo_in, eg_in, *parts = refs[:5]
    gvec, bo, eg, gw1, gw2 = refs[5:10]
    vecs, sem = refs[10:16], refs[16]
    copies = []
    for k, (src, dst) in enumerate(((bo_in, bo), (eg_in, eg))):
        for m in range(src.shape[0]):
            for e in range(2):
                copies.append(
                    pltpu.make_async_copy(src.at[m, :, :, pl.ds(e * C, C)], dst.at[m, :, e], sem.at[k, m, e])
                )
                copies[-1].start()
    for ref, (v, columns) in zip(parts, PARTS):
        for i in range(3):
            for at, j in enumerate(columns):
                row = (i * len(columns) + at) * C
                (gw1, gw2)[v][i * 3 + j] = ref[row : row + C].astype(f32)
    for k, ref in enumerate(vecs):
        ref[...] = gvec[k : k + 1]
    for copy in copies:
        copy.wait()


def solution(mesh):
    n = mesh.shape["dp"]
    pieces = [piece_rows(part_rows(x), n) for x in range(3)]

    def per_device(inputs, channel_mean, channel_std, cotangent, conv_w1, conv_b1, bn_gain1, bn_shift1, conv_w2, conv_b2, bn_gain2, bn_shift2):
        micro, _, H, W, _ = inputs.shape
        half = micro // 2
        Q = H // 2
        field = (micro, Q, 2, W, C)
        pairs = (micro, Q, W, 2 * C)
        anywhere = pl.BlockSpec(memory_space=pl.ANY)
        vmem = pl.BlockSpec(memory_space=pltpu.VMEM)
        D = pltpu.SemaphoreType.DMA
        V = pltpu.VMEM
        whole_parts = [V((size * own, C), bf16) for size, own in pieces]
        mid = pl.pallas_call(
            functools.partial(kernel, n),
            out_shape=[
                V(pairs, bf16),
                V(pairs, bf16),
                *whole_parts,
                V((8, C), f32),
            ],
            in_specs=[anywhere, anywhere, vmem, vmem, anywhere, vmem, vmem, vmem, anywhere, vmem, vmem, vmem],
            out_specs=[vmem] * 6,
            scratch_shapes=[
                V((half, Q, W, 2 * C), bf16),
                V((half, Q, W, 2 * C), bf16),
                V((4 * half, Q + 1, W, 2 * C), bf16),
                V((3, Q + 1, W, 2 * C), bf16),
                V((3, Q + 1, W, 2 * C), bf16),
                V((4, half, Q, W, 2 * C), f32),
                V((4, 3, 2, 2 * C, 2 * C), bf16),
                V((4, 3, 2, 2 * C, 2 * C), bf16),
                V((4, 4 * C, 6 * C), f32),
                V((2, 8, C), f32),
                V((4, half, 8, C), f32),
                V((2, 8, C), f32),
                V((8, C), f32),
                V((2 * half, 4, C), f32),
                V((2 * half, n, 4, C), f32),
                *whole_parts,
                *whole_parts,
                *whole_parts,
                *[V((n, size, C), bf16) for size, _ in pieces],
                D((2 * half,)),
                D((2,)),
                D((3,)),
                D((3,)),
                D((2 * half,)),
                D((2 * half,)),
                D((4,)),
                D((4,)),
                D((4,)),
                D((3, 4)),
                D((3, 4)),
                D((2,)),
            ],
            compiler_params=pltpu.CompilerParams(
                collective_id=0, has_side_effects=True, vmem_limit_bytes=VMEM_LIMIT
            ),
        )(
            inputs.reshape(field),
            cotangent.reshape(field),
            channel_mean[None],
            channel_std[None],
            conv_w1.reshape(9, 2, C // 2, C),
            conv_b1,
            bn_gain1,
            bn_shift1,
            conv_w2.reshape(9, 2, C // 2, C),
            conv_b2,
            bn_gain2,
            bn_shift2,
        )
        bo, eg, gw1, gw2, *vecs = pl.pallas_call(
            writer,
            out_shape=[
                jax.ShapeDtypeStruct(field, bf16),
                jax.ShapeDtypeStruct(field, bf16),
                jax.ShapeDtypeStruct((9, C, C), f32),
                jax.ShapeDtypeStruct((9, C, C), f32),
            ]
            + [jax.ShapeDtypeStruct((1, C), f32)] * 6,
            in_specs=[vmem] * 6,
            out_specs=[anywhere, anywhere] + [vmem] * 8,
            scratch_shapes=[D((2, micro, 2))],
            compiler_params=pltpu.CompilerParams(vmem_limit_bytes=8 * 2**20),
        )(*[pltpu.with_memory_space_constraint(v, pltpu.VMEM) for v in mid])
        whole = (1, micro, 1, H, W, C)
        kernel_shape = (1, 3, 3, C, C)
        return (
            bo.reshape(whole),
            eg.reshape(whole),
            gw1.reshape(kernel_shape),
            vecs[0],
            vecs[1],
            vecs[2],
            gw2.reshape(kernel_shape),
            vecs[3],
            vecs[4],
            vecs[5],
        )

    in_specs = (
        P(None, "dp", None, None, None),
        P(),
        P(),
        P(None, "dp", None, None, None),
        P("section", None, None, None, None),
        P("section", None),
        P("section", None),
        P("section", None),
        P("section", None, None, None, None),
        P("section", None),
        P("section", None),
        P("section", None),
    )
    out_specs = (
        P("section", None, "dp", None, None, None),
        P("section", None, "dp", None, None, None),
        P("section", None, None, None, None),
        P("section", None),
        P("section", None),
        P("section", None),
        P("section", None, None, None, None),
        P("section", None),
        P("section", None),
        P("section", None),
    )
    return jax.shard_map(per_device, mesh=mesh, in_specs=in_specs, out_specs=out_specs, check_vma=False)
```

```python
import functools

import jax
import jax.numpy as jnp
from jax import lax
from jax.experimental import pallas as pl
from jax.experimental.pallas import tpu as pltpu
from jax.sharding import PartitionSpec as P

norm_eps = 1e-05
MESH = pl.DeviceIdType.MESH
bf16 = jnp.bfloat16
f32 = jnp.float32
C = 128
VMEM_LIMIT = 55 * 2**20


def dot(a, b):
    return jnp.dot(a, b, preferred_element_type=f32)


def fold_rows(v):
    return jnp.sum(v, axis=0, keepdims=True)


PARTS = ((1, (0, 1, 2)), (0, (0, 1)), (0, (2,)))


def part_rows(x):
    return 3 * len(PARTS[x][1]) * C


def plane_of(n):
    plane = min(d for d in range(1, n + 1) if n % d == 0 and d * d >= n)
    planes = n // plane
    return plane, planes, min(2, max(1, planes // 2))


def piece_rows(rows, n):
    plane, _, owning = plane_of(n)
    owners = plane * owning
    return -(-rows // owners // 16) * 16, owners


def kernel(n, *refs):
    (
        inp, cot, mean, std, w1, b1, g1, s1, w2, b2, g2, s2,
        bo, eg, GO0, GO1, GO2, gvec,
        XIN, COT, XC, LOW0, LOW1, HS, WF, WD, ACC, PV, ST, VACC, VR,
        MSG, SLOT, PS0, PS1, PS2, GR0, GR1, GR2, GP0, GP1, GP2,
        isem, wlsem, wssem, wrsem, msend, mrecv, olsem, ossem, orsem, gsend, grecv, vsem,
    ) = refs
    micro = inp.shape[0]
    half = micro // 2
    Q = inp.shape[1]
    W = inp.shape[3]
    rows = Q * W
    count = float(2 * rows * n)

    plane, all_planes, owning = plane_of(n)
    first_plane = (all_planes - owning) // 2

    me = lax.axis_index("dp")
    my_plane, my_line = me // plane, me % plane
    my_piece = my_line * owning + my_plane - first_plane
    is_owner = (my_plane >= first_plane) & (my_plane < first_plane + owning)
    sec = lax.axis_index("section")
    sib = 1 - sec

    def peer(d):
        return {"dp": lax.rem(me + d, n)}

    def every_peer(body):
        if n <= 16:
            for d in range(1, n):
                body(d)
        else:
            lax.fori_loop(1, n, lambda d, carry: (body(d), carry)[1], 0)

    def wait(ref, sem):
        pltpu.make_async_copy(ref, ref, sem).wait()

    def to_sibling(src, dst, send, recv):
        pltpu.make_async_remote_copy(
            src, dst, send, recv, device_id={"section": sib}, device_id_type=MESH
        ).start()

    barrier = pltpu.get_barrier_semaphore()
    pl.semaphore_signal(barrier, inc=1, device_id={"section": sib}, device_id_type=MESH)
    every_peer(lambda d: pl.semaphore_signal(barrier, inc=1, device_id=peer(d), device_id_type=MESH))

    def raw(b, v):
        return XC.at[3 * half + 2 * b + v, pl.ds(0, 9)]

    def raw_tap(b, v, k):
        tap = raw(b, v)[k]
        return jnp.concatenate([tap[:, :C], tap[:, C:]], axis=0)

    for v, ref in enumerate((w1, w2)):
        for e in range(2):
            pltpu.make_async_copy(ref.at[:, e], raw(sec, v).at[:, :, pl.ds(e * C, C)], wlsem.at[v]).start()
    for src, dst, at in ((inp, XIN, 0), (cot, COT, half)):
        for m in range(half):
            for e in range(2):
                pltpu.make_async_copy(
                    src.at[sec * half + m, :, e], dst.at[m, :, :, pl.ds(e * C, C)], isem.at[at + m]
                ).start()

    for v, ref in enumerate((b1, g1, s1, b2, g2, s2)):
        PV[sec, v : v + 1] = ref[...]

    halo = jnp.zeros((W, C), bf16)
    for j in range(3):
        LOW0[j, 0, :, 0:C] = halo
        LOW0[j, Q, :, C : 2 * C] = halo
    LOW1[...] = jnp.zeros(LOW1.shape, bf16)

    def zero_halo(i, carry):
        XC[i, 0, :, 0:C] = halo
        XC[i, Q, :, C : 2 * C] = halo
        return carry

    lax.fori_loop(0, 3 * half, zero_halo, 0)
    empty = jnp.zeros((C, C), bf16)
    for i in range(4):
        ACC[i] = jnp.zeros(ACC.shape[1:], f32)
        for j in range(3):
            for ref in (WF, WD):
                ref[i, j, 0, 0:C, C : 2 * C] = empty
                ref[i, j, 1, C : 2 * C, 0:C] = empty
    VACC[...] = jnp.zeros(VACC.shape, f32)
    for ref in (PS0, PS1, PS2):
        ref[...] = jnp.zeros(ref.shape, bf16)

    pl.semaphore_wait(barrier, n)

    to_sibling(PV.at[sec], PV.at[sec], wssem.at[2], wrsem.at[2])
    for v in range(2):
        wait(raw(sec, v), wlsem.at[v])
        to_sibling(raw(sec, v), raw(sec, v), wssem.at[v], wrsem.at[v])

    def blocks():
        for j in range(3):
            for t in range(2):
                for s in range(2):
                    for e in range(2):
                        i = 2 * t + s - e
                        if 0 <= i <= 2:
                            yield i, j, t, slice(s * C, s * C + C), slice(e * C, e * C + C)

    def prep_forward(b, v):
        for i, j, t, r, c in blocks():
            WF[b * 2 + v, j, t, r, c] = (raw_tap(b, v, i * 3 + j).astype(f32) * 0.5).astype(bf16)

    def prep_backward(b, v):
        for i, j, t, r, c in blocks():
            WD[b * 2 + v, j, t, r, c] = raw_tap(b, v, (2 - i) * 3 + 2 - j).T

    def vec(b, v):
        return PV[b, v : v + 1]

    def send_sums(i, *sums):
        for r, v in enumerate(sums):
            MSG[i, r : r + 1] = v
        SLOT[i, me] = MSG[i]
        every_peer(
            lambda d: pltpu.make_async_remote_copy(
                MSG.at[i], SLOT.at[i, me], msend.at[i], mrecv.at[i], device_id=peer(d), device_id_type=MESH
            ).start()
        )

    def sum_slots(i):
        total = SLOT[i, 0]
        for d in range(1, n):
            total = total + SLOT[i, d]
        return total

    def take_sums(i):
        if n > 1:
            many = SLOT.at[i, pl.ds(0, n - 1)]
            wait(many, mrecv.at[i])
            wait(many, msend.at[i])
        return sum_slots(i)

    def norm_forward(b, v, m, total):
        mu = total[0:1] / count
        rstd = lax.rsqrt(total[1:2] / count - mu * mu + norm_eps)
        ST[b * 2 + v, m, 0:1] = mu
        ST[b * 2 + v, m, 1:2] = rstd
        sc = vec(b, 1 + 3 * v) * rstd
        return sc, vec(b, 2 + 3 * v) - mu * sc

    def norm_backward(b, v, m, shift_sum, prod_sum):
        mu = ST[b * 2 + v, m, 0:1]
        rstd = ST[b * 2 + v, m, 1:2]
        gain_sum = rstd * (prod_sum - mu * shift_sum)
        VACC[b, 3 * v + 1 : 3 * v + 2] += gain_sum
        VACC[b, 3 * v + 2 : 3 * v + 3] += shift_sum
        ca = vec(b, 1 + 3 * v) * rstd
        cc = -ca * rstd * gain_sum / count
        cb = -ca * shift_sum / count - cc * mu
        return ca, cb, cc

    def spot(q, e):
        return q + e, slice(None), slice((1 - e) * C, (2 - e) * C)

    def put(trio, q, e, v):
        for j, ref in enumerate(trio):
            ref[spot(q, e)] = (v if j == 1 else pltpu.roll(v, 1 if j == 0 else W - 1, 0)).astype(bf16)

    def get_all(center):
        both = [center[0:Q, :, C : 2 * C], center[1 : Q + 1, :, 0:C]]
        return jnp.concatenate(both, axis=-1).reshape(rows, 2 * C)

    def conv(trio, w):
        acc = None
        for j, ref in enumerate(trio):
            for t in range(2):
                d = dot(ref[t : t + Q].reshape(rows, 2 * C), w[j, t])
                acc = d if acc is None else acc + d
        return acc

    def wgrad(i, center, trio, which=(0, 1, 2)):
        left = jnp.concatenate([center[0:Q].reshape(rows, 2 * C), center[1 : Q + 1].reshape(rows, 2 * C)], axis=-1)
        for j in which:
            ACC[i, :, j * 2 * C : (j + 1) * 2 * C] += lax.dot_general(
                left, get_all(trio[j]), (((0,), (0,)), ((), ())), preferred_element_type=f32
            )

    def planes():
        for q in range(Q):
            for e in range(2):
                yield q, e, (q, slice(None), slice(e * C, e * C + C))

    def part(r, q, e):
        return r[q * W : (q + 1) * W, e * C : (e + 1) * C]

    def add8(total, v):
        return total + jnp.sum(v.reshape(-1, 8, C), axis=0)

    zero8 = jnp.zeros((8, C), f32)

    def act_of(h):
        return h + h * jnp.tanh(h)

    mean1 = mean[...]
    inv1 = 1.0 / std[...]

    def standard(m, at):
        return (XIN[(m, *at)].astype(f32) - mean1) * inv1

    def after_conv(b, v, m, r, cots):
        bias = vec(b, 3 * v) * 0.5
        t0, t1, t2, t3 = zero8, zero8, zero8, zero8
        for q, e, at in planes():
            h = part(r, q, e) + bias
            HS[(b * 2 + v, m, *at)] = h
            act = act_of(h)
            t0, t1 = add8(t0, act), add8(t1, act * act)
            if cots:
                dy = COT[(m, *at)].astype(f32)
                t2, t3 = add8(t2, dy), add8(t3, dy * act)
        sums = (fold_rows(t0), fold_rows(t1))
        if cots:
            sums += (fold_rows(t2), fold_rows(t3))
        return sums

    def send_block(views, b, t):
        @pl.when(sec == b)
        def _():
            for src, dst in views:
                pltpu.make_async_copy(src, dst, olsem.at[t]).start()

        @pl.when(sec != b)
        def _():
            for src, dst in views:
                to_sibling(src, dst, ossem.at[t], orsem.at[t])

    def sent_blocks(out, b, t):
        many = out.at[pl.ds(0, half)]

        @pl.when(sec == b)
        def _():
            wait(many, olsem.at[t])

        @pl.when(sec != b)
        def _():
            wait(many, ossem.at[t])

    def came_blocks(out, b, t):
        @pl.when(sec == b)
        def _():
            wait(out.at[pl.ds(0, half)], orsem.at[t])

    def xc(b, v, m):
        return XC.at[(b * 2 + v) * half + m]

    def trio_of(center):
        return LOW0.at[0], center, LOW0.at[2]

    low0 = tuple(LOW0.at[j] for j in range(3))
    low1 = tuple(LOW1.at[j] for j in range(3))

    def slot(stage, m):
        return (stage % 2) * half + m

    def stage0(m, carry):
        wait(XIN.at[m], isem.at[m])
        trio = trio_of(xc(0, 0, m))
        for q, e, at in planes():
            put(trio, q, e, standard(m, at))
        send_sums(slot(0, m), *after_conv(0, 0, m, conv(trio, WF.at[0]), False))
        return carry

    def stage_norm1(b, stage, m):
        sc, sh = norm_forward(b, 0, m, take_sums(slot(stage - 1, m)))
        if b == 1:
            wait(COT.at[m], isem.at[half + m])
        trio = trio_of(xc(b, 1, m))
        for q, e, at in planes():
            put(trio, q, e, act_of(HS[(b * 2, m, *at)]) * sc + sh)
        send_sums(slot(stage, m), *after_conv(b, 1, m, conv(trio, WF.at[b * 2 + 1]), b == 1))

    def stage1(m, carry):
        stage_norm1(0, 1, m)
        return carry

    def stage2(m, carry):
        sc, sh = norm_forward(0, 1, m, take_sums(slot(1, m)))
        center = xc(1, 0, m)
        trio = trio_of(center)
        for q, e, at in planes():
            put(trio, q, e, standard(m, at) + (act_of(HS[(1, m, *at)]) * sc + sh))
        send_sums(slot(2, m), *after_conv(1, 0, m, conv(trio, WF.at[2]), False))
        send_block(
            [
                (center.at[pl.ds(e, Q), :, pl.ds((1 - e) * C, C)], bo.at[sec * half + m, :, :, pl.ds(e * C, C)])
                for e in range(2)
            ],
            0,
            0,
        )
        return carry

    def stage3(m, carry):
        stage_norm1(1, 3, m)
        return carry

    def back_plane(trio, i, m, q, e, at, dy, coef):
        ca, cb, cc = coef
        h = HS[(i, m, *at)]
        u = 1.0 + jnp.tanh(h)
        act = h * u
        dp = (ca * dy + (cc * act + cb)) * (act + (0.5 * u) * (1.0 - act))
        put(trio, q, e, dp)
        return act, dp

    def step_e(b, stage, m, trio, before):
        total = take_sums(slot(stage - 1, m))
        if b == 1:
            sc, sh = norm_forward(1, 1, m, total)
            coef = norm_backward(1, 1, m, total[2:3], total[3:4])
        else:
            coef = norm_backward(0, 1, m, total[0:1], total[1:2])
            VACC[1, 0:1] += total[2:3]
        t0, t1, t2 = zero8, zero8, zero8
        i = b * 2 + 1
        wgrad(*before)
        for q, e, at in planes():
            act, dp = back_plane(trio, i, m, q, e, at, COT[(m, *at)].astype(f32), coef)
            t2 = add8(t2, dp)
            if b == 1:
                final = xc(1, 0, m)[spot(q, e)].astype(f32) + (act * sc + sh)
                XIN[(m, *at)] = final.astype(bf16)
        r = conv(trio, WD.at[i])
        for q, e, at in planes():
            dn = part(r, q, e)
            HS[(i, m, *at)] = dn
            t0, t1 = add8(t0, dn), add8(t1, dn * act_of(HS[(b * 2, m, *at)]))
        send_sums(slot(stage, m), fold_rows(t0), fold_rows(t1), fold_rows(t2))
        if b == 1:
            send_block([(XIN.at[m], bo.at[sec * half + m])], 1, 1)

    def coef_f(b, stage, m):
        total = take_sums(slot(stage - 1, m))
        VACC[b, 3:4] += total[2:3]
        return norm_backward(b, 0, m, total[0:1], total[1:2])

    def low_f(trio, b, m, coef):
        t2 = zero8
        for q, e, at in planes():
            t2 = add8(t2, back_plane(trio, b * 2, m, q, e, at, HS[(b * 2 + 1, m, *at)], coef)[1])
        return t2

    def step_f(b, stage, m, trio, before):
        coef = coef_f(1, stage, m)
        wgrad(*before)
        t2 = low_f(trio, 1, m, coef)
        r = conv(trio, WD.at[2])
        t0, t1 = zero8, zero8
        for q, e, at in planes():
            da = (COT[(m, *at)].astype(f32) + part(r, q, e)).astype(bf16)
            COT[(m, *at)] = da
            da = da.astype(f32)
            t0, t1 = add8(t0, da), add8(t1, da * act_of(HS[(1, m, *at)]))
        send_sums(slot(stage, m), fold_rows(t0), fold_rows(t1), fold_rows(t2))
        send_block([(COT.at[m], eg.at[sec * half + m])], 1, 2)

    def back_stage(step, b, stage, own, last, after):
        def hooks(k, odd):
            for m, body in after:
                if m % 2 == odd:
                    pl.when(k == m // 2)(body)

        def pair(k, carry):
            m = 2 * k
            first = lax.div(1, k + 1)
            i = own + (last - own) * first
            x = own * half + m - 1 + ((last - own) * half + half) * first
            step(b, stage, m, low0, (i, XC.at[x], low1))
            hooks(k, 0)
            step(b, stage, m + 1, low1, (own, xc(own // 2, own % 2, m), low0))
            hooks(k, 1)
            return carry

        lax.fori_loop(0, half // 2, pair, 0)

    def buffers(x):
        return ((PS0, PS1, PS2)[x], (GR0, GR1, GR2)[x], (GR0, GR1, GR2)[x], (GP0, GP1, GP2)[x], (GO0, GO1, GO2)[x])

    def taps(b, x):
        v, columns = PARTS[x]
        a = ACC.at[b * 2 + v]
        for i in range(3):
            for at, j in enumerate(columns):
                out = None
                for t in range(2):
                    for s in range(2):
                        e = 2 * t + s - i
                        if 0 <= e <= 1:
                            r = (2 * t + s) * C
                            c = ((2 - j) * 2 + e) * C
                            d = a[r : r + C, c : c + C]
                            out = d if out is None else out + d
                yield (i * len(columns) + at) * C, out

    def to_pair(b, x):
        ps, _, gr, _, _ = buffers(x)

        @pl.when(sec != b)
        def _():
            for row, val in taps(b, x):
                ps[row : row + C] = val.astype(bf16)
            to_sibling(ps, gr, gsend.at[x, 0], grecv.at[x, 0])

    def piece_size(x):
        return buffers(x)[3].shape[1]

    owners = plane * owning

    def piece(ref, x, p):
        size = piece_size(x)
        return ref.at[pl.ds(pl.multiple_of(p * size, 16), size)]

    def span(ref, x, k):
        return ref.at[pl.ds(0, k * piece_size(x))]

    def when_owner(b, mine, other):
        pl.when((sec == b) & is_owner)(mine)
        pl.when((sec == b) & jnp.logical_not(is_owner))(other)

    def to_owners(b, x):
        _, gs, gr, gp, _ = buffers(x)

        @pl.when(sec == b)
        def _():
            wait(gr, grecv.at[x, 0])
            for row, val in taps(b, x):
                gs[row : row + C] = (val + gr[row : row + C].astype(f32)).astype(bf16)

        def send(p):
            to = (first_plane + p % owning) * plane + p // owning
            pltpu.make_async_remote_copy(
                piece(gs, x, p), gp.at[me], gsend.at[x, 1], grecv.at[x, 1], device_id={"dp": to}, device_id_type=MESH
            ).start()

        def mine():
            for d in range(1, owners):
                send(lax.rem(my_piece + d, owners))
            gp[me] = piece(gs, x, my_piece)[...]

        def other():
            for d in range(owners):
                send(lax.rem(me + d, owners))

        when_owner(b, mine, other)

    def to_all(b, x, direct):
        _, gs, _, gp, go = buffers(x)

        def mine():
            if n > 1:
                wait(gp.at[pl.ds(0, n - 1)], grecv.at[x, 1])
            if owners > 1:
                wait(span(gs, x, owners - 1), gsend.at[x, 1])
            total = gp[0].astype(f32)
            for d in range(1, n):
                total = total + gp[d].astype(f32)
            at = piece(go, x, my_piece)
            at[...] = total.astype(bf16)

            def send(to):
                pltpu.make_async_remote_copy(
                    at, at, gsend.at[x, 2], grecv.at[x, 2], device_id=to, device_id_type=MESH
                ).start()

            if direct:
                every_peer(lambda d: send(peer(d)))
            else:
                for d in range(1, all_planes):
                    send({"dp": lax.rem(my_plane + d, all_planes) * plane + my_line})

        when_owner(b, mine, lambda: wait(span(gs, x, owners), gsend.at[x, 1]))

    def got_pieces(b, x, k):
        go = buffers(x)[4]

        def mine():
            if k > 1:
                wait(span(go, x, k - 1), grecv.at[x, 2])

        when_owner(b, mine, lambda: wait(span(go, x, k), grecv.at[x, 2]))

    def spread(b, x):
        go = buffers(x)[4]
        got_pieces(b, x, owning)
        size = piece_size(x) * owning
        at = go.at[pl.ds(pl.multiple_of(my_line * size, 16), size)]

        @pl.when(sec == b)
        def _():
            for d in range(1, plane):
                pltpu.make_async_remote_copy(
                    at, at, gsend.at[x, 3], grecv.at[x, 3],
                    device_id={"dp": my_plane * plane + lax.rem(my_line + d, plane)}, device_id_type=MESH,
                ).start()

    def finish(b, x, direct):
        ps, _, _, gp, go = buffers(x)
        copies = n - 1 if direct else all_planes - 1
        if direct:
            got_pieces(b, x, owners)

        @pl.when(sec == b)
        def _():
            if not direct and plane > 1:
                many = span(go, x, owning * (plane - 1))
                wait(many, grecv.at[x, 3])
                wait(many, gsend.at[x, 3])

        if copies > 0:
            pl.when((sec == b) & is_owner)(lambda: wait(gp.at[pl.ds(0, copies)], gsend.at[x, 2]))

        @pl.when(sec != b)
        def _():
            wait(ps, gsend.at[x, 0])

    @pl.when(sec != 0)
    def _():
        wait(raw(0, 0), wrsem.at[0])

    prep_forward(0, 0)
    wait(PV.at[0], wrsem.at[2])
    lax.fori_loop(0, half, stage0, 0)

    @pl.when(sec == 0)
    def _():
        wait(raw(0, 0), wrsem.at[0])

    wait(raw(0, 1), wrsem.at[1])
    for v in range(2):
        wait(raw(0, 0), wssem.at[v])
    wait(PV.at[0], wssem.at[2])
    prep_forward(0, 1)
    prep_backward(0, 0)
    lax.fori_loop(0, half, stage1, 0)
    prep_forward(1, 0)
    prep_backward(0, 1)
    lax.fori_loop(0, half, stage2, 0)
    prep_forward(1, 1)
    prep_backward(1, 1)
    prep_backward(1, 0)
    lax.fori_loop(3 * half, 4 * half, zero_halo, 0)
    lax.fori_loop(0, half, stage3, 0)
    w1_parts = (1, 2)
    back_stage(step_e, 1, 4, 3, 2, [])
    back_stage(step_f, 1, 5, 2, 3, [(0, lambda: to_pair(1, 0)), (1, lambda: to_owners(1, 0))])

    def every_part(phase, b):
        for x in w1_parts:
            phase(b, x)

    back_stage(
        step_e,
        0,
        6,
        1,
        2,
        [
            (0, lambda: every_part(to_pair, 1)),
            (1, lambda: every_part(to_owners, 1)),
            (1, lambda: to_all(1, 0, False)),
        ],
    )
    sent_blocks(bo, 0, 0)

    def last_trio(m):
        return xc(1, 1, m), xc(0, 1, m), xc(1, 0, m)

    for m in range(half):
        coef = coef_f(0, 7, m)
        if m == 0:
            wgrad(1, xc(0, 1, half - 1), low1)
        else:
            wgrad(0, xc(0, 0, m - 1), last_trio(m - 1), (2, 1))
        send_sums(slot(7, m), fold_rows(low_f(last_trio(m), 0, m, coef)))
        if m == 0:
            to_pair(0, 0)
        if m == 1:
            to_owners(0, 0)
            spread(1, 0)
        if m == half - 1:
            for x in w1_parts:
                to_all(1, x, False)
    wgrad(0, xc(0, 0, half - 1), last_trio(half - 1), (2, 1))
    to_pair(0, 1)

    def last_column(m, carry):
        wgrad(0, xc(0, 0, m), last_trio(m), (0,))
        return carry

    lax.fori_loop(0, half, last_column, 0)
    to_pair(0, 2)
    to_owners(0, 1)
    sent_blocks(eg, 1, 2)

    def stage8(m, carry):
        r = conv(last_trio(m), WD.at[0])
        for q, e, at in planes():
            da = (COT[(m, *at)].astype(f32) + part(r, q, e)) * inv1
            COT[(m, *at)] = da.astype(bf16)
        send_block([(COT.at[m], eg.at[sec * half + m])], 0, 3)

        @pl.when(m == 0)
        def _():
            to_owners(0, 2)

        @pl.when(m == 1)
        def _():
            to_all(0, 0, False)
            every_part(spread, 1)

        return carry

    lax.fori_loop(0, half, stage8, 0)

    for m in range(half):
        VACC[0, 0:1] += take_sums(slot(7, m))[0:1]
    to_sibling(VACC.at[sib], VR, vsem.at[0], vsem.at[1])
    spread(0, 0)
    for x in w1_parts:
        to_all(0, x, True)
    wait(VR, vsem.at[1])
    wait(VR, vsem.at[0])
    gvec[...] = VACC[sec] + VR[...]
    sent_blocks(bo, 1, 1)
    sent_blocks(eg, 0, 3)
    came_blocks(bo, 0, 0)
    came_blocks(bo, 1, 1)
    came_blocks(eg, 1, 2)
    came_blocks(eg, 0, 3)
    for b in (1, 0):
        for x in range(3):
            finish(b, x, b == 0 and x > 0)


def writer(*refs):
    bo_in, eg_in, *parts = refs[:5]
    gvec, bo, eg, gw1, gw2 = refs[5:10]
    vecs, sem = refs[10:16], refs[16]
    copies = []
    for k, (src, dst) in enumerate(((bo_in, bo), (eg_in, eg))):
        for m in range(src.shape[0]):
            for e in range(2):
                copies.append(
                    pltpu.make_async_copy(src.at[m, :, :, pl.ds(e * C, C)], dst.at[m, :, e], sem.at[k, m, e])
                )
                copies[-1].start()
    for ref, (v, columns) in zip(parts, PARTS):
        for i in range(3):
            for at, j in enumerate(columns):
                row = (i * len(columns) + at) * C
                (gw1, gw2)[v][i * 3 + j] = ref[row : row + C].astype(f32)
    for k, ref in enumerate(vecs):
        ref[...] = gvec[k : k + 1]
    for copy in copies:
        copy.wait()


def solution(mesh):
    n = mesh.shape["dp"]
    pieces = [piece_rows(part_rows(x), n) for x in range(3)]

    def per_device(inputs, channel_mean, channel_std, cotangent, conv_w1, conv_b1, bn_gain1, bn_shift1, conv_w2, conv_b2, bn_gain2, bn_shift2):
        micro, _, H, W, _ = inputs.shape
        half = micro // 2
        Q = H // 2
        field = (micro, Q, 2, W, C)
        pairs = (micro, Q, W, 2 * C)
        anywhere = pl.BlockSpec(memory_space=pl.ANY)
        vmem = pl.BlockSpec(memory_space=pltpu.VMEM)
        D = pltpu.SemaphoreType.DMA
        V = pltpu.VMEM
        whole_parts = [V((size * own, C), bf16) for size, own in pieces]
        mid = pl.pallas_call(
            functools.partial(kernel, n),
            out_shape=[
                V(pairs, bf16),
                V(pairs, bf16),
                *whole_parts,
                V((8, C), f32),
            ],
            in_specs=[anywhere, anywhere, vmem, vmem, anywhere, vmem, vmem, vmem, anywhere, vmem, vmem, vmem],
            out_specs=[vmem] * 6,
            scratch_shapes=[
                V((half, Q, W, 2 * C), bf16),
                V((half, Q, W, 2 * C), bf16),
                V((4 * half, Q + 1, W, 2 * C), bf16),
                V((3, Q + 1, W, 2 * C), bf16),
                V((3, Q + 1, W, 2 * C), bf16),
                V((4, half, Q, W, 2 * C), f32),
                V((4, 3, 2, 2 * C, 2 * C), bf16),
                V((4, 3, 2, 2 * C, 2 * C), bf16),
                V((4, 4 * C, 6 * C), f32),
                V((2, 8, C), f32),
                V((4, half, 8, C), f32),
                V((2, 8, C), f32),
                V((8, C), f32),
                V((2 * half, 4, C), f32),
                V((2 * half, n, 4, C), f32),
                *whole_parts,
                *whole_parts,
                *[V((n, size, C), bf16) for size, _ in pieces],
                D((2 * half,)),
                D((2,)),
                D((3,)),
                D((3,)),
                D((2 * half,)),
                D((2 * half,)),
                D((4,)),
                D((4,)),
                D((4,)),
                D((3, 4)),
                D((3, 4)),
                D((2,)),
            ],
            compiler_params=pltpu.CompilerParams(
                collective_id=0, has_side_effects=True, vmem_limit_bytes=VMEM_LIMIT
            ),
        )(
            inputs.reshape(field),
            cotangent.reshape(field),
            channel_mean[None],
            channel_std[None],
            conv_w1.reshape(9, 2, C // 2, C),
            conv_b1,
            bn_gain1,
            bn_shift1,
            conv_w2.reshape(9, 2, C // 2, C),
            conv_b2,
            bn_gain2,
            bn_shift2,
        )
        bo, eg, gw1, gw2, *vecs = pl.pallas_call(
            writer,
            out_shape=[
                jax.ShapeDtypeStruct(field, bf16),
                jax.ShapeDtypeStruct(field, bf16),
                jax.ShapeDtypeStruct((9, C, C), f32),
                jax.ShapeDtypeStruct((9, C, C), f32),
            ]
            + [jax.ShapeDtypeStruct((1, C), f32)] * 6,
            in_specs=[vmem] * 6,
            out_specs=[anywhere, anywhere] + [vmem] * 8,
            scratch_shapes=[D((2, micro, 2))],
            compiler_params=pltpu.CompilerParams(vmem_limit_bytes=8 * 2**20),
        )(*[pltpu.with_memory_space_constraint(v, pltpu.VMEM) for v in mid])
        whole = (1, micro, 1, H, W, C)
        kernel_shape = (1, 3, 3, C, C)
        return (
            bo.reshape(whole),
            eg.reshape(whole),
            gw1.reshape(kernel_shape),
            vecs[0],
            vecs[1],
            vecs[2],
            gw2.reshape(kernel_shape),
            vecs[3],
            vecs[4],
            vecs[5],
        )

    in_specs = (
        P(None, "dp", None, None, None),
        P(),
        P(),
        P(None, "dp", None, None, None),
        P("section", None, None, None, None),
        P("section", None),
        P("section", None),
        P("section", None),
        P("section", None, None, None, None),
        P("section", None),
        P("section", None),
        P("section", None),
    )
    out_specs = (
        P("section", None, "dp", None, None, None),
        P("section", None, "dp", None, None, None),
        P("section", None, None, None, None),
        P("section", None),
        P("section", None),
        P("section", None),
        P("section", None, None, None, None),
        P("section", None),
        P("section", None),
        P("section", None),
    )
    return jax.shard_map(per_device, mesh=mesh, in_specs=in_specs, out_specs=out_specs, check_vma=False)
```

```python
import functools

import jax
import jax.numpy as jnp
from jax import lax
from jax.experimental import pallas as pl
from jax.experimental.pallas import tpu as pltpu
from jax.sharding import PartitionSpec as P

norm_eps = 1e-05
MESH = pl.DeviceIdType.MESH
bf16 = jnp.bfloat16
f32 = jnp.float32
C = 128
VMEM_LIMIT = 55 * 2**20


def dot(a, b):
    return jnp.dot(a, b, preferred_element_type=f32)


def fold_rows(v):
    return jnp.sum(v, axis=0, keepdims=True)


PARTS = ((1, (0, 1, 2)), (0, (0, 1)), (0, (2,)))


def part_rows(x):
    return 3 * len(PARTS[x][1]) * C


def plane_of(n):
    plane = min(d for d in range(1, n + 1) if n % d == 0 and d * d >= n)
    planes = n // plane
    return plane, planes, min(2, max(1, planes // 2))


def piece_rows(rows, n):
    plane, _, owning = plane_of(n)
    owners = plane * owning
    return -(-rows // owners // 16) * 16, owners


def kernel(n, *refs):
    (
        inp, cot, mean, std, w1, b1, g1, s1, w2, b2, g2, s2,
        bo, eg, GO0, GO1, GO2, gvec,
        XIN, COT, XC, LOW0, LOW1, HS, WF, WD, ACC, PV, ST, VACC, VR,
        MSG, SLOT, PS0, PS1, PS2, GR0, GR1, GR2, GP0, GP1, GP2,
        isem, wlsem, wssem, wrsem, msend, mrecv, olsem, ossem, orsem, gsend, grecv, vsem,
    ) = refs
    micro = inp.shape[0]
    half = micro // 2
    Q = inp.shape[1]
    W = inp.shape[3]
    rows = Q * W
    count = float(2 * rows * n)

    plane, all_planes, owning = plane_of(n)
    first_plane = (all_planes - owning) // 2

    me = lax.axis_index("dp")
    my_plane, my_line = me // plane, me % plane
    my_piece = my_line * owning + my_plane - first_plane
    is_owner = (my_plane >= first_plane) & (my_plane < first_plane + owning)
    sec = lax.axis_index("section")
    sib = 1 - sec

    def peer(d):
        return {"dp": lax.rem(me + d, n)}

    def every_peer(body):
        if n <= 16:
            for d in range(1, n):
                body(d)
        else:
            lax.fori_loop(1, n, lambda d, carry: (body(d), carry)[1], 0)

    def wait(ref, sem):
        pltpu.make_async_copy(ref, ref, sem).wait()

    def to_sibling(src, dst, send, recv):
        pltpu.make_async_remote_copy(
            src, dst, send, recv, device_id={"section": sib}, device_id_type=MESH
        ).start()

    barrier = pltpu.get_barrier_semaphore()
    pl.semaphore_signal(barrier, inc=1, device_id={"section": sib}, device_id_type=MESH)
    every_peer(lambda d: pl.semaphore_signal(barrier, inc=1, device_id=peer(d), device_id_type=MESH))

    def raw(b, v):
        return XC.at[3 * half + 2 * b + v, pl.ds(0, 9)]

    def raw_tap(b, v, k):
        tap = raw(b, v)[k]
        return jnp.concatenate([tap[:, :C], tap[:, C:]], axis=0)

    for v, ref in enumerate((w1, w2)):
        for e in range(2):
            pltpu.make_async_copy(ref.at[:, e], raw(sec, v).at[:, :, pl.ds(e * C, C)], wlsem.at[v]).start()
    for src, dst, at in ((inp, XIN, 0), (cot, COT, half)):
        for m in range(half):
            for e in range(2):
                pltpu.make_async_copy(
                    src.at[sec * half + m, :, e], dst.at[m, :, :, pl.ds(e * C, C)], isem.at[at + m]
                ).start()

    for v, ref in enumerate((b1, g1, s1, b2, g2, s2)):
        PV[sec, v : v + 1] = ref[...]

    halo = jnp.zeros((W, C), bf16)
    for j in range(3):
        LOW0[j, 0, :, 0:C] = halo
        LOW0[j, Q, :, C : 2 * C] = halo
    LOW1[...] = jnp.zeros(LOW1.shape, bf16)

    def zero_halo(i, carry):
        XC[i, 0, :, 0:C] = halo
        XC[i, Q, :, C : 2 * C] = halo
        return carry

    lax.fori_loop(0, 3 * half, zero_halo, 0)
    empty = jnp.zeros((C, C), bf16)
    for i in range(4):
        ACC[i] = jnp.zeros(ACC.shape[1:], f32)
        for j in range(3):
            for ref in (WF, WD):
                ref[i, j, 0, 0:C, C : 2 * C] = empty
                ref[i, j, 1, C : 2 * C, 0:C] = empty
    VACC[...] = jnp.zeros(VACC.shape, f32)
    for ref in (PS0, PS1, PS2):
        ref[...] = jnp.zeros(ref.shape, bf16)

    pl.semaphore_wait(barrier, n)

    to_sibling(PV.at[sec], PV.at[sec], wssem.at[2], wrsem.at[2])
    for v in range(2):
        wait(raw(sec, v), wlsem.at[v])
        to_sibling(raw(sec, v), raw(sec, v), wssem.at[v], wrsem.at[v])

    def blocks():
        for j in range(3):
            for t in range(2):
                for s in range(2):
                    for e in range(2):
                        i = 2 * t + s - e
                        if 0 <= i <= 2:
                            yield i, j, t, slice(s * C, s * C + C), slice(e * C, e * C + C)

    def prep_forward(b, v):
        for i, j, t, r, c in blocks():
            WF[b * 2 + v, j, t, r, c] = (raw_tap(b, v, i * 3 + j).astype(f32) * 0.5).astype(bf16)

    def prep_backward(b, v):
        for i, j, t, r, c in blocks():
            WD[b * 2 + v, j, t, r, c] = raw_tap(b, v, (2 - i) * 3 + 2 - j).T

    def vec(b, v):
        return PV[b, v : v + 1]

    def send_sums(i, *sums):
        for r, v in enumerate(sums):
            MSG[i, r : r + 1] = v
        SLOT[i, me] = MSG[i]
        every_peer(
            lambda d: pltpu.make_async_remote_copy(
                MSG.at[i], SLOT.at[i, me], msend.at[i], mrecv.at[i], device_id=peer(d), device_id_type=MESH
            ).start()
        )

    def sum_slots(i):
        total = SLOT[i, 0]
        for d in range(1, n):
            total = total + SLOT[i, d]
        return total

    def take_sums(i):
        if n > 1:
            many = SLOT.at[i, pl.ds(0, n - 1)]
            wait(many, mrecv.at[i])
            wait(many, msend.at[i])
        return sum_slots(i)

    def norm_forward(b, v, m, total):
        mu = total[0:1] / count
        rstd = lax.rsqrt(total[1:2] / count - mu * mu + norm_eps)
        ST[b * 2 + v, m, 0:1] = mu
        ST[b * 2 + v, m, 1:2] = rstd
        sc = vec(b, 1 + 3 * v) * rstd
        return sc, vec(b, 2 + 3 * v) - mu * sc

    def norm_backward(b, v, m, shift_sum, prod_sum):
        mu = ST[b * 2 + v, m, 0:1]
        rstd = ST[b * 2 + v, m, 1:2]
        gain_sum = rstd * (prod_sum - mu * shift_sum)
        VACC[b, 3 * v + 1 : 3 * v + 2] += gain_sum
        VACC[b, 3 * v + 2 : 3 * v + 3] += shift_sum
        ca = vec(b, 1 + 3 * v) * rstd
        cc = -ca * rstd * gain_sum / count
        cb = -ca * shift_sum / count - cc * mu
        return ca, cb, cc

    def spot(q, e):
        return q + e, slice(None), slice((1 - e) * C, (2 - e) * C)

    def put(trio, q, e, v):
        for j, ref in enumerate(trio):
            ref[spot(q, e)] = (v if j == 1 else pltpu.roll(v, 1 if j == 0 else W - 1, 0)).astype(bf16)

    def get_all(center):
        both = [center[0:Q, :, C : 2 * C], center[1 : Q + 1, :, 0:C]]
        return jnp.concatenate(both, axis=-1).reshape(rows, 2 * C)

    def conv(trio, w):
        acc = None
        for j, ref in enumerate(trio):
            for t in range(2):
                d = dot(ref[t : t + Q].reshape(rows, 2 * C), w[j, t])
                acc = d if acc is None else acc + d
        return acc

    def wgrad(i, center, trio, which=(0, 1, 2)):
        left = jnp.concatenate([center[0:Q].reshape(rows, 2 * C), center[1 : Q + 1].reshape(rows, 2 * C)], axis=-1)
        for j in which:
            ACC[i, :, j * 2 * C : (j + 1) * 2 * C] += lax.dot_general(
                left, get_all(trio[j]), (((0,), (0,)), ((), ())), preferred_element_type=f32
            )

    def planes():
        for q in range(Q):
            for e in range(2):
                yield q, e, (q, slice(None), slice(e * C, e * C + C))

    def part(r, q, e):
        return r[q * W : (q + 1) * W, e * C : (e + 1) * C]

    def add8(total, v):
        return total + jnp.sum(v.reshape(-1, 8, C), axis=0)

    zero8 = jnp.zeros((8, C), f32)

    def act_of(h):
        return h + h * jnp.tanh(h)

    mean1 = mean[...]
    inv1 = 1.0 / std[...]

    def standard(m, at):
        return (XIN[(m, *at)].astype(f32) - mean1) * inv1

    def after_conv(b, v, m, r, cots):
        bias = vec(b, 3 * v) * 0.5
        t0, t1, t2, t3 = zero8, zero8, zero8, zero8
        for q, e, at in planes():
            h = part(r, q, e) + bias
            HS[(b * 2 + v, m, *at)] = h
            act = act_of(h)
            t0, t1 = add8(t0, act), add8(t1, act * act)
            if cots:
                dy = COT[(m, *at)].astype(f32)
                t2, t3 = add8(t2, dy), add8(t3, dy * act)
        sums = (fold_rows(t0), fold_rows(t1))
        if cots:
            sums += (fold_rows(t2), fold_rows(t3))
        return sums

    def send_block(views, b, t):
        @pl.when(sec == b)
        def _():
            for src, dst in views:
                pltpu.make_async_copy(src, dst, olsem.at[t]).start()

        @pl.when(sec != b)
        def _():
            for src, dst in views:
                to_sibling(src, dst, ossem.at[t], orsem.at[t])

    def sent_blocks(out, b, t):
        many = out.at[pl.ds(0, half)]

        @pl.when(sec == b)
        def _():
            wait(many, olsem.at[t])

        @pl.when(sec != b)
        def _():
            wait(many, ossem.at[t])

    def came_blocks(out, b, t):
        @pl.when(sec == b)
        def _():
            wait(out.at[pl.ds(0, half)], orsem.at[t])

    def xc(b, v, m):
        return XC.at[(b * 2 + v) * half + m]

    def trio_of(center):
        return LOW0.at[0], center, LOW0.at[2]

    low0 = tuple(LOW0.at[j] for j in range(3))
    low1 = tuple(LOW1.at[j] for j in range(3))

    def slot(stage, m):
        return (stage % 2) * half + m

    def stage0(m, carry):
        wait(XIN.at[m], isem.at[m])
        trio = trio_of(xc(0, 0, m))
        for q, e, at in planes():
            put(trio, q, e, standard(m, at))
        send_sums(slot(0, m), *after_conv(0, 0, m, conv(trio, WF.at[0]), False))
        return carry

    def stage_norm1(b, stage, m):
        sc, sh = norm_forward(b, 0, m, take_sums(slot(stage - 1, m)))
        if b == 1:
            wait(COT.at[m], isem.at[half + m])
        trio = trio_of(xc(b, 1, m))
        for q, e, at in planes():
            put(trio, q, e, act_of(HS[(b * 2, m, *at)]) * sc + sh)
        send_sums(slot(stage, m), *after_conv(b, 1, m, conv(trio, WF.at[b * 2 + 1]), b == 1))

    def stage1(m, carry):
        stage_norm1(0, 1, m)
        return carry

    def stage2(m, carry):
        sc, sh = norm_forward(0, 1, m, take_sums(slot(1, m)))
        center = xc(1, 0, m)
        trio = trio_of(center)
        for q, e, at in planes():
            put(trio, q, e, standard(m, at) + (act_of(HS[(1, m, *at)]) * sc + sh))
        send_sums(slot(2, m), *after_conv(1, 0, m, conv(trio, WF.at[2]), False))
        send_block(
            [
                (center.at[pl.ds(e, Q), :, pl.ds((1 - e) * C, C)], bo.at[sec * half + m, :, :, pl.ds(e * C, C)])
                for e in range(2)
            ],
            0,
            0,
        )
        return carry

    def stage3(m, carry):
        stage_norm1(1, 3, m)
        return carry

    def back_plane(trio, i, m, q, e, at, dy, coef):
        ca, cb, cc = coef
        h = HS[(i, m, *at)]
        u = 1.0 + jnp.tanh(h)
        act = h * u
        dp = (ca * dy + (cc * act + cb)) * (act + (0.5 * u) * (1.0 - act))
        put(trio, q, e, dp)
        return act, dp

    def step_e(b, stage, m, trio, before):
        total = take_sums(slot(stage - 1, m))
        if b == 1:
            sc, sh = norm_forward(1, 1, m, total)
            coef = norm_backward(1, 1, m, total[2:3], total[3:4])
        else:
            coef = norm_backward(0, 1, m, total[0:1], total[1:2])
            VACC[1, 0:1] += total[2:3]
        t0, t1, t2 = zero8, zero8, zero8
        i = b * 2 + 1
        wgrad(*before)
        for q, e, at in planes():
            act, dp = back_plane(trio, i, m, q, e, at, COT[(m, *at)].astype(f32), coef)
            t2 = add8(t2, dp)
            if b == 1:
                final = xc(1, 0, m)[spot(q, e)].astype(f32) + (act * sc + sh)
                XIN[(m, *at)] = final.astype(bf16)
        r = conv(trio, WD.at[i])
        for q, e, at in planes():
            dn = part(r, q, e)
            HS[(i, m, *at)] = dn
            t0, t1 = add8(t0, dn), add8(t1, dn * act_of(HS[(b * 2, m, *at)]))
        send_sums(slot(stage, m), fold_rows(t0), fold_rows(t1), fold_rows(t2))
        if b == 1:
            send_block([(XIN.at[m], bo.at[sec * half + m])], 1, 1)

    def coef_f(b, stage, m):
        total = take_sums(slot(stage - 1, m))
        VACC[b, 3:4] += total[2:3]
        return norm_backward(b, 0, m, total[0:1], total[1:2])

    def low_f(trio, b, m, coef):
        t2 = zero8
        for q, e, at in planes():
            t2 = add8(t2, back_plane(trio, b * 2, m, q, e, at, HS[(b * 2 + 1, m, *at)], coef)[1])
        return t2

    def step_f(b, stage, m, trio, before):
        coef = coef_f(1, stage, m)
        wgrad(*before)
        t2 = low_f(trio, 1, m, coef)
        r = conv(trio, WD.at[2])
        t0, t1 = zero8, zero8
        for q, e, at in planes():
            da = (COT[(m, *at)].astype(f32) + part(r, q, e)).astype(bf16)
            COT[(m, *at)] = da
            da = da.astype(f32)
            t0, t1 = add8(t0, da), add8(t1, da * act_of(HS[(1, m, *at)]))
        send_sums(slot(stage, m), fold_rows(t0), fold_rows(t1), fold_rows(t2))
        send_block([(COT.at[m], eg.at[sec * half + m])], 1, 2)

    def back_stage(step, b, stage, own, last, after):
        def hooks(k, odd):
            for m, body in after:
                if m % 2 == odd:
                    pl.when(k == m // 2)(body)

        def pair(k, carry):
            m = 2 * k
            first = lax.div(1, k + 1)
            i = own + (last - own) * first
            x = own * half + m - 1 + ((last - own) * half + half) * first
            step(b, stage, m, low0, (i, XC.at[x], low1))
            hooks(k, 0)
            step(b, stage, m + 1, low1, (own, xc(own // 2, own % 2, m), low0))
            hooks(k, 1)
            return carry

        lax.fori_loop(0, half // 2, pair, 0)

    def buffers(x):
        return ((PS0, PS1, PS2)[x], (GR0, GR1, GR2)[x], (GR0, GR1, GR2)[x], (GP0, GP1, GP2)[x], (GO0, GO1, GO2)[x])

    def taps(b, x):
        v, columns = PARTS[x]
        a = ACC.at[b * 2 + v]
        for i in range(3):
            for at, j in enumerate(columns):
                out = None
                for t in range(2):
                    for s in range(2):
                        e = 2 * t + s - i
                        if 0 <= e <= 1:
                            r = (2 * t + s) * C
                            c = ((2 - j) * 2 + e) * C
                            d = a[r : r + C, c : c + C]
                            out = d if out is None else out + d
                yield (i * len(columns) + at) * C, out

    def to_pair(b, x):
        ps, _, gr, _, _ = buffers(x)

        @pl.when(sec != b)
        def _():
            for row, val in taps(b, x):
                ps[row : row + C] = val.astype(bf16)
            to_sibling(ps, gr, gsend.at[x, 0], grecv.at[x, 0])

    def piece_size(x):
        return buffers(x)[3].shape[1]

    owners = plane * owning

    def piece(ref, x, p):
        size = piece_size(x)
        return ref.at[pl.ds(pl.multiple_of(p * size, 16), size)]

    def span(ref, x, k):
        return ref.at[pl.ds(0, k * piece_size(x))]

    def when_owner(b, mine, other):
        pl.when((sec == b) & is_owner)(mine)
        pl.when((sec == b) & jnp.logical_not(is_owner))(other)

    def to_owners(b, x):
        _, gs, gr, gp, _ = buffers(x)

        @pl.when(sec == b)
        def _():
            wait(gr, grecv.at[x, 0])
            for row, val in taps(b, x):
                gs[row : row + C] = (val + gr[row : row + C].astype(f32)).astype(bf16)

        def send(p):
            to = (first_plane + p % owning) * plane + p // owning
            pltpu.make_async_remote_copy(
                piece(gs, x, p), gp.at[me], gsend.at[x, 1], grecv.at[x, 1], device_id={"dp": to}, device_id_type=MESH
            ).start()

        def mine():
            for d in range(1, owners):
                send(lax.rem(my_piece + d, owners))
            gp[me] = piece(gs, x, my_piece)[...]

        def other():
            for d in range(owners):
                send(lax.rem(me + d, owners))

        when_owner(b, mine, other)

    def to_all(b, x, direct):
        _, gs, _, gp, go = buffers(x)

        def mine():
            if n > 1:
                wait(gp.at[pl.ds(0, n - 1)], grecv.at[x, 1])
            if owners > 1:
                wait(span(gs, x, owners - 1), gsend.at[x, 1])
            total = gp[0].astype(f32)
            for d in range(1, n):
                total = total + gp[d].astype(f32)
            at = piece(go, x, my_piece)
            at[...] = total.astype(bf16)

            def send(to):
                pltpu.make_async_remote_copy(
                    at, at, gsend.at[x, 2], grecv.at[x, 2], device_id=to, device_id_type=MESH
                ).start()

            if direct:
                every_peer(lambda d: send(peer(d)))
            else:
                for d in range(1, all_planes):
                    send({"dp": lax.rem(my_plane + d, all_planes) * plane + my_line})

        when_owner(b, mine, lambda: wait(span(gs, x, owners), gsend.at[x, 1]))

    def got_pieces(b, x, k):
        go = buffers(x)[4]

        def mine():
            if k > 1:
                wait(span(go, x, k - 1), grecv.at[x, 2])

        when_owner(b, mine, lambda: wait(span(go, x, k), grecv.at[x, 2]))

    def spread(b, x):
        go = buffers(x)[4]
        got_pieces(b, x, owning)
        size = piece_size(x) * owning
        at = go.at[pl.ds(pl.multiple_of(my_line * size, 16), size)]

        @pl.when(sec == b)
        def _():
            for d in range(1, plane):
                pltpu.make_async_remote_copy(
                    at, at, gsend.at[x, 3], grecv.at[x, 3],
                    device_id={"dp": my_plane * plane + lax.rem(my_line + d, plane)}, device_id_type=MESH,
                ).start()

    def finish(b, x, direct):
        ps, _, _, gp, go = buffers(x)
        copies = n - 1 if direct else all_planes - 1
        if direct:
            got_pieces(b, x, owners)

        @pl.when(sec == b)
        def _():
            if not direct and plane > 1:
                many = span(go, x, owning * (plane - 1))
                wait(many, grecv.at[x, 3])
                wait(many, gsend.at[x, 3])

        if copies > 0:
            pl.when((sec == b) & is_owner)(lambda: wait(gp.at[pl.ds(0, copies)], gsend.at[x, 2]))

        @pl.when(sec != b)
        def _():
            wait(ps, gsend.at[x, 0])

    @pl.when(sec != 0)
    def _():
        wait(raw(0, 0), wrsem.at[0])

    prep_forward(0, 0)
    wait(PV.at[0], wrsem.at[2])
    lax.fori_loop(0, half, stage0, 0)

    @pl.when(sec == 0)
    def _():
        wait(raw(0, 0), wrsem.at[0])

    wait(raw(0, 1), wrsem.at[1])
    for v in range(2):
        wait(raw(0, 0), wssem.at[v])
    wait(PV.at[0], wssem.at[2])
    prep_forward(0, 1)
    prep_backward(0, 0)
    lax.fori_loop(0, half, stage1, 0)
    prep_forward(1, 0)
    prep_backward(0, 1)
    lax.fori_loop(0, half, stage2, 0)
    prep_forward(1, 1)
    prep_backward(1, 1)
    prep_backward(1, 0)
    lax.fori_loop(3 * half, 4 * half, zero_halo, 0)
    lax.fori_loop(0, half, stage3, 0)
    w1_parts = (1, 2)
    back_stage(step_e, 1, 4, 3, 2, [])
    back_stage(step_f, 1, 5, 2, 3, [(0, lambda: to_pair(1, 0)), (1, lambda: to_owners(1, 0))])

    def every_part(phase, b):
        for x in w1_parts:
            phase(b, x)

    back_stage(
        step_e,
        0,
        6,
        1,
        2,
        [
            (0, lambda: every_part(to_pair, 1)),
            (1, lambda: every_part(to_owners, 1)),
            (1, lambda: to_all(1, 0, False)),
        ],
    )
    sent_blocks(bo, 0, 0)

    def last_trio(m):
        return xc(1, 1, m), xc(0, 1, m), xc(1, 0, m)

    for m in range(half):
        coef = coef_f(0, 7, m)
        if m == 0:
            wgrad(1, xc(0, 1, half - 1), low1)
        else:
            wgrad(0, xc(0, 0, m - 1), last_trio(m - 1), (2, 1))
        send_sums(slot(7, m), fold_rows(low_f(last_trio(m), 0, m, coef)))
        if m == 0:
            to_pair(0, 0)
        if m == 1:
            to_owners(0, 0)
            spread(1, 0)
        if m == half - 1:
            for x in w1_parts:
                to_all(1, x, False)
    wgrad(0, xc(0, 0, half - 1), last_trio(half - 1), (2, 1))
    to_pair(0, 1)

    def last_column(m, carry):
        wgrad(0, xc(0, 0, m), last_trio(m), (0,))
        return carry

    lax.fori_loop(0, half, last_column, 0)
    to_pair(0, 2)
    to_owners(0, 1)
    sent_blocks(eg, 1, 2)

    def stage8(m, carry):
        r = conv(last_trio(m), WD.at[0])
        for q, e, at in planes():
            da = (COT[(m, *at)].astype(f32) + part(r, q, e)) * inv1
            COT[(m, *at)] = da.astype(bf16)
        send_block([(COT.at[m], eg.at[sec * half + m])], 0, 3)

        @pl.when(m == 0)
        def _():
            to_owners(0, 2)

        @pl.when(m == 0)
        def _():
            to_all(0, 0, False)
            every_part(spread, 1)

        return carry

    lax.fori_loop(0, half, stage8, 0)

    for m in range(half):
        VACC[0, 0:1] += take_sums(slot(7, m))[0:1]
    to_sibling(VACC.at[sib], VR, vsem.at[0], vsem.at[1])
    spread(0, 0)
    for x in w1_parts:
        to_all(0, x, True)
    wait(VR, vsem.at[1])
    wait(VR, vsem.at[0])
    gvec[...] = VACC[sec] + VR[...]
    sent_blocks(bo, 1, 1)
    sent_blocks(eg, 0, 3)
    came_blocks(bo, 0, 0)
    came_blocks(bo, 1, 1)
    came_blocks(eg, 1, 2)
    came_blocks(eg, 0, 3)
    for b in (1, 0):
        for x in range(3):
            finish(b, x, b == 0 and x > 0)


def writer(*refs):
    bo_in, eg_in, *parts = refs[:5]
    gvec, bo, eg, gw1, gw2 = refs[5:10]
    vecs, sem = refs[10:16], refs[16]
    copies = []
    for k, (src, dst) in enumerate(((bo_in, bo), (eg_in, eg))):
        for m in range(src.shape[0]):
            for e in range(2):
                copies.append(
                    pltpu.make_async_copy(src.at[m, :, :, pl.ds(e * C, C)], dst.at[m, :, e], sem.at[k, m, e])
                )
                copies[-1].start()
    for ref, (v, columns) in zip(parts, PARTS):
        for i in range(3):
            for at, j in enumerate(columns):
                row = (i * len(columns) + at) * C
                (gw1, gw2)[v][i * 3 + j] = ref[row : row + C].astype(f32)
    for k, ref in enumerate(vecs):
        ref[...] = gvec[k : k + 1]
    for copy in copies:
        copy.wait()


def solution(mesh):
    n = mesh.shape["dp"]
    pieces = [piece_rows(part_rows(x), n) for x in range(3)]

    def per_device(inputs, channel_mean, channel_std, cotangent, conv_w1, conv_b1, bn_gain1, bn_shift1, conv_w2, conv_b2, bn_gain2, bn_shift2):
        micro, _, H, W, _ = inputs.shape
        half = micro // 2
        Q = H // 2
        field = (micro, Q, 2, W, C)
        pairs = (micro, Q, W, 2 * C)
        anywhere = pl.BlockSpec(memory_space=pl.ANY)
        vmem = pl.BlockSpec(memory_space=pltpu.VMEM)
        D = pltpu.SemaphoreType.DMA
        V = pltpu.VMEM
        whole_parts = [V((size * own, C), bf16) for size, own in pieces]
        mid = pl.pallas_call(
            functools.partial(kernel, n),
            out_shape=[
                V(pairs, bf16),
                V(pairs, bf16),
                *whole_parts,
                V((8, C), f32),
            ],
            in_specs=[anywhere, anywhere, vmem, vmem, anywhere, vmem, vmem, vmem, anywhere, vmem, vmem, vmem],
            out_specs=[vmem] * 6,
            scratch_shapes=[
                V((half, Q, W, 2 * C), bf16),
                V((half, Q, W, 2 * C), bf16),
                V((4 * half, Q + 1, W, 2 * C), bf16),
                V((3, Q + 1, W, 2 * C), bf16),
                V((3, Q + 1, W, 2 * C), bf16),
                V((4, half, Q, W, 2 * C), f32),
                V((4, 3, 2, 2 * C, 2 * C), bf16),
                V((4, 3, 2, 2 * C, 2 * C), bf16),
                V((4, 4 * C, 6 * C), f32),
                V((2, 8, C), f32),
                V((4, half, 8, C), f32),
                V((2, 8, C), f32),
                V((8, C), f32),
                V((2 * half, 4, C), f32),
                V((2 * half, n, 4, C), f32),
                *whole_parts,
                *whole_parts,
                *[V((n, size, C), bf16) for size, _ in pieces],
                D((2 * half,)),
                D((2,)),
                D((3,)),
                D((3,)),
                D((2 * half,)),
                D((2 * half,)),
                D((4,)),
                D((4,)),
                D((4,)),
                D((3, 4)),
                D((3, 4)),
                D((2,)),
            ],
            compiler_params=pltpu.CompilerParams(
                collective_id=0, has_side_effects=True, vmem_limit_bytes=VMEM_LIMIT
            ),
        )(
            inputs.reshape(field),
            cotangent.reshape(field),
            channel_mean[None],
            channel_std[None],
            conv_w1.reshape(9, 2, C // 2, C),
            conv_b1,
            bn_gain1,
            bn_shift1,
            conv_w2.reshape(9, 2, C // 2, C),
            conv_b2,
            bn_gain2,
            bn_shift2,
        )
        bo, eg, gw1, gw2, *vecs = pl.pallas_call(
            writer,
            out_shape=[
                jax.ShapeDtypeStruct(field, bf16),
                jax.ShapeDtypeStruct(field, bf16),
                jax.ShapeDtypeStruct((9, C, C), f32),
                jax.ShapeDtypeStruct((9, C, C), f32),
            ]
            + [jax.ShapeDtypeStruct((1, C), f32)] * 6,
            in_specs=[vmem] * 6,
            out_specs=[anywhere, anywhere] + [vmem] * 8,
            scratch_shapes=[D((2, micro, 2))],
            compiler_params=pltpu.CompilerParams(vmem_limit_bytes=8 * 2**20),
        )(*[pltpu.with_memory_space_constraint(v, pltpu.VMEM) for v in mid])
        whole = (1, micro, 1, H, W, C)
        kernel_shape = (1, 3, 3, C, C)
        return (
            bo.reshape(whole),
            eg.reshape(whole),
            gw1.reshape(kernel_shape),
            vecs[0],
            vecs[1],
            vecs[2],
            gw2.reshape(kernel_shape),
            vecs[3],
            vecs[4],
            vecs[5],
        )

    in_specs = (
        P(None, "dp", None, None, None),
        P(),
        P(),
        P(None, "dp", None, None, None),
        P("section", None, None, None, None),
        P("section", None),
        P("section", None),
        P("section", None),
        P("section", None, None, None, None),
        P("section", None),
        P("section", None),
        P("section", None),
    )
    out_specs = (
        P("section", None, "dp", None, None, None),
        P("section", None, "dp", None, None, None),
        P("section", None, None, None, None),
        P("section", None),
        P("section", None),
        P("section", None),
        P("section", None, None, None, None),
        P("section", None),
        P("section", None),
        P("section", None),
    )
    return jax.shard_map(per_device, mesh=mesh, in_specs=in_specs, out_specs=out_specs, check_vma=False)
```
